128 devices in a mesh: group: 4 (over z), mp: 8 (over x_hi, y), dp: 4 (over x_lo, core).
Axes of the slice: x: 4 (x_hi: 2, x_lo: 2; x = x_hi * 2 + x_lo), y: 4, z: 4, core: 2. Of those that a mesh axis runs over, the one named last changes fastest.
Arguments:
- teacher_panels: bfloat16 [8, 4, 2, 1024, 6144], P('group', 'dp', None, None, 'mp'), may hold values from -64 to 64
- owner_plan: int32 [2], replicated, may hold values from 0 to 7, as said below
- head_map: int32 [48, 1], replicated, may hold values from 0 to 15
- student_input: bfloat16 [4, 2, 4, 1024, 1024], P('group', None, 'dp'), may hold values from -64 to 64
- student_weights: bfloat16 [4, 2, 1024, 1024], P('group', None, 'dp', 'mp'), may hold values from -1 to 1
Outputs:
- weight_grads: float32 [4, 2, 1024, 1024], P('group', None, 'dp', 'mp')
The draws below stay inside these ranges and needn't reach their ends.
Inputs may be any that keep to these rules, and one draw needn't show every extreme that they name: `owner_plan`: distinct store slots, one for each of the 2 micro-batches; the last slot is always among them.
All inputs are finite; a program needn't handle non-finite values.
Results may differ from the reference program's by a relative error of at most 0.0027.
Values may be sent and summed in bfloat16 or wider, within the bound.
No kernel may reach another device: no remote copies, remote signals or barrier semaphores. Data moves between devices by JAX's collectives and lax.ppermute only.
A program may use at most 128 MiB of HBM per device.

```python
import jax
import jax.numpy as jnp
from jax import lax

HT = 48
HDT = 128
HS = 16
HDS = 64
TOK = 1024
NMB = 2
D = 1024
IMAGES = 4
STORE = 8
N_GROUP = 4


def draw_teacher_panels(key, part):
    key = jax.random.fold_in(key, 17)
    feature_width = HT * HDT
    subkeys = jax.random.split(key, STORE * IMAGES)

    def one_panel(subkey):
        base_key = jax.random.fold_in(subkey, 0)
        return jnp.clip(jax.random.normal(base_key, (2, TOK, feature_width), jnp.float32), -6.0, 6.0)
    panels = jax.vmap(one_panel)(subkeys)
    return panels.reshape(STORE, IMAGES, 2, TOK, feature_width).astype(jnp.bfloat16)


def draw_owner_plan(key, part):
    key = jax.random.fold_in(key, 5)
    pick_key, order_key = jax.random.split(key)
    others = jax.random.permutation(pick_key, STORE - 1)[:NMB - 1].astype(jnp.int32)
    slots = jnp.concatenate([others, jnp.full((1,), STORE - 1, jnp.int32)])
    return jax.random.permutation(order_key, slots).astype(jnp.int32)


def draw_student_input(key, part):
    key = jax.random.fold_in(key, 23)
    subkeys = jax.random.split(key, N_GROUP * NMB * IMAGES)

    def one_image(subkey):
        base_key = jax.random.fold_in(subkey, 0)
        return jnp.clip(jax.random.normal(base_key, (TOK, D), jnp.float32), -6.0, 6.0)
    images = jax.vmap(one_image)(subkeys)
    return images.reshape(N_GROUP, NMB, IMAGES, TOK, D).astype(jnp.bfloat16)


def draw_student_weights(key, part):
    key = jax.random.fold_in(key, 29)
    base_key, other_key = jax.random.split(key)
    base = jnp.clip(jax.random.normal(base_key, (N_GROUP, D, D), jnp.float32), -6.0, 6.0)
    other = jnp.clip(jax.random.normal(other_key, (N_GROUP, D, D), jnp.float32), -6.0, 6.0)
    paired = other
    stacked = jnp.stack([base, paired], axis=1) * D ** (-0.5)
    return stacked.astype(jnp.bfloat16)


def picks_of(key, rows, number_of, top, lift):
    sequence = jax.random.permutation(jax.random.fold_in(key, 1), number_of)
    pull = sequence
    for power in range(3):
        pull = pull * pull // number_of
    pull = pull * lift // number_of
    tickets = jax.random.randint(jax.random.fold_in(key, 2), (rows, number_of), 0, 4096) + pull
    sure = jax.random.permutation(jax.random.fold_in(key, 3), rows)[jnp.arange(number_of) % rows]
    tickets = jnp.where(jnp.arange(rows)[:, None] == sure[None, :], 1 << 14, tickets)
    merit = tickets * number_of + jnp.arange(number_of)
    return lax.top_k(merit.astype(jnp.int32), top)[1].astype(jnp.int32)


def setup_inputs(seed: int = 0) -> dict:
    seeds = jax.random.split(jax.random.key(seed), 6)
    return {
        "teacher_panels": draw_teacher_panels(jax.random.fold_in(seeds[5], 71), 0),
        "owner_plan": draw_owner_plan(jax.random.fold_in(seeds[5], 71), 0),
        "head_map": picks_of(seeds[2], HT, HS, 1, 1024),
        "student_input": draw_student_input(jax.random.fold_in(seeds[5], 71), 0),
        "student_weights": draw_student_weights(jax.random.fold_in(seeds[5], 71), 0),
    }


def normalize_rows(scores):
    row_peak = jnp.max(scores, axis=-1, keepdims=True)
    shifted = jnp.exp(scores - row_peak)
    return shifted / jnp.sum(shifted, axis=-1, keepdims=True)


def reference(teacher_panels, owner_plan, head_map, student_input, student_weights):
    teacher_scale = HDT ** -0.5
    student_scale = HDS ** -0.5
    anchor = jnp.int32(0)
    targets = head_map[:, 0].astype(jnp.int32)
    weight_grads = jnp.zeros((N_GROUP, 2, D, D), jnp.float32)
    for micro_batch in range(NMB):
        slot_index = owner_plan[micro_batch].astype(jnp.int32)
        panels = lax.dynamic_index_in_dim(teacher_panels, slot_index, 0, keepdims=False)
        inputs = student_input[:, micro_batch]

        def image_step(image_index, grad_sum):
            image_index = image_index.astype(jnp.int32)
            picture = lax.dynamic_index_in_dim(panels, image_index, 0, keepdims=False)
            image_rows = lax.dynamic_index_in_dim(inputs, image_index, 1, keepdims=False)

            def head_step(teacher_head, grad_inner):
                teacher_head = teacher_head.astype(jnp.int32)
                feature_start = (teacher_head * HDT).astype(jnp.int32)
                teacher_query = lax.dynamic_slice(picture[0], (anchor, feature_start), (TOK, HDT))
                teacher_key = lax.dynamic_slice(picture[1], (anchor, feature_start), (TOK, HDT))
                relation = normalize_rows(jnp.dot(teacher_query, teacher_key.T, preferred_element_type=jnp.float32) * teacher_scale)
                column_start = (targets[teacher_head] * HDS).astype(jnp.int32)

                def one_student(rows_in, weights_in):
                    query_cols = lax.dynamic_slice(weights_in[0], (anchor, column_start), (D, HDS))
                    key_cols = lax.dynamic_slice(weights_in[1], (anchor, column_start), (D, HDS))
                    student_query = jnp.dot(rows_in, query_cols, preferred_element_type=jnp.float32).astype(jnp.bfloat16)
                    student_key = jnp.dot(rows_in, key_cols, preferred_element_type=jnp.float32).astype(jnp.bfloat16)
                    student_relation = normalize_rows(jnp.dot(student_query, student_key.T, preferred_element_type=jnp.float32) * student_scale)
                    mismatch = (student_relation - relation).astype(jnp.bfloat16)
                    grad_query = (jnp.dot(mismatch, student_key, preferred_element_type=jnp.float32) * student_scale).astype(jnp.bfloat16)
                    grad_key = (jnp.dot(mismatch.T, student_query, preferred_element_type=jnp.float32) * student_scale).astype(jnp.bfloat16)
                    return jnp.stack([jnp.dot(rows_in.T, grad_query, preferred_element_type=jnp.float32),
                                      jnp.dot(rows_in.T, grad_key, preferred_element_type=jnp.float32)])

                update = jax.vmap(one_student)(image_rows, student_weights)
                corner = (anchor, anchor, anchor, column_start)
                current = lax.dynamic_slice(grad_inner, corner, (N_GROUP, 2, D, HDS))
                return lax.dynamic_update_slice(grad_inner, current + update, corner)

            return lax.fori_loop(0, HT, head_step, grad_sum)

        weight_grads = lax.fori_loop(0, IMAGES, image_step, weight_grads)
    return weight_grads
```

```python
import functools

import jax
import jax.numpy as jnp
from jax import lax
from jax.experimental import pallas as pl
from jax.experimental.pallas import tpu as pltpu
from jax.sharding import PartitionSpec as P

HDT = 128
HDS = 64
LOG2E = 1.4426950408889634
QUERIES = 256
HALF = 512
PIECE = 64
LAG = 2
NT = (((1,), (1,)), ((), ()))
NN = (((1,), (0,)), ((), ()))


def dot(a, b, dims):
    return lax.dot_general(a, b, dims, preferred_element_type=jnp.float32)


def relation_kernel(head, batch, relays, place_ref, store_ref, *refs):
    arrivals = refs[:2 * relays]
    pair_ref, x_hbm, out_ref = refs[2 * relays:2 * relays + 3]
    panel, x_ref, q_ref, k_ref, turned, exp_s, exp_t, mix, acc, grads, sems = refs[2 * relays + 3:]
    tokens = k_ref.shape[0]

    @pl.when(place_ref[0, batch] == 0)
    def _():
        for part in range(2):
            held = store_ref.at[place_ref[1, batch], 0, part, :, pl.ds(head * HDT, HDT)]
            pltpu.make_async_copy(held, panel.at[part], sems.at[part]).start()

    for d in range(relays):
        @pl.when(place_ref[0, batch] == d + 1)
        def _():
            for part in range(2):
                pltpu.make_async_copy(arrivals[2 * d + part], panel.at[part], sems.at[part]).start()

    fetch = pltpu.make_async_copy(x_hbm.at[batch], x_ref, sems.at[2])
    fetch.start()
    pair = pair_ref[0]
    q_ref[...] = pair[:, :HDS] * jnp.bfloat16(HDS ** -0.5)
    k_ref[...] = pair[:, HDS:]
    turned[...] = pair.T
    turned[:HDS] = turned[:HDS] * jnp.bfloat16(HDS ** -0.5)
    for part in range(2):
        pltpu.make_async_copy(arrivals[part], panel.at[part], sems.at[part]).wait()
    blocks = tokens // QUERIES
    halves = tokens // HALF
    pieces = HALF // PIECE
    rates = (LOG2E, HDT ** -0.5 * LOG2E)

    def exps(block, half):
        cols = pl.ds(block * QUERIES, QUERIES)
        rows = pl.ds(half * HALF, HALF)
        both = (dot(k_ref[rows, :], turned[:HDS, cols], NN), dot(panel[1, rows, :], panel[0, cols, :], NT))
        stats = []
        for p in range(pieces):
            here = pl.ds(half * HALF + p * PIECE, PIECE)
            stat = []
            for score, rate, store in zip(both, rates, (exp_s, exp_t)):
                x = score[p * PIECE:(p + 1) * PIECE].reshape(PIECE // 8, 8, QUERIES)
                peak = jnp.max(x, axis=0)
                e = jnp.exp2((x - peak[None]) * rate)
                store[block % 2, here, :] = e.reshape(PIECE, QUERIES)
                stat.append((peak, jnp.sum(e, axis=0)))
            stats.append(stat)
        return stats

    def factors(stats):
        out = []
        for side in range(2):
            peaks = [stat[side][0] for stat in stats]
            top = peaks[0]
            for peak in peaks[1:]:
                top = jnp.maximum(top, peak)
            top = jnp.max(top, axis=0, keepdims=True)
            scale = [jnp.exp2((peak - top) * rates[side]) for peak in peaks]
            total = scale[0] * stats[0][side][1]
            for f, stat in zip(scale[1:], stats[1:]):
                total = total + f * stat[side][1]
            norm = 1.0 / jnp.sum(total, axis=0, keepdims=True)
            out.append([f * norm for f in scale])
        return out

    stats = [stat for half in range(halves) for stat in exps(0, half)]
    for block in range(blocks):
        slot = block % 2
        cols = pl.ds(block * QUERIES, QUERIES)
        scale_s, scale_t = factors(stats)
        stats = []
        for half in range(halves):
            if block + 1 < blocks:
                stats += exps(block + 1, half)
            for p in range(half * pieces, (half + 1) * pieces):
                here = pl.ds(p * PIECE, PIECE)
                s = exp_s[slot, here, :].reshape(PIECE // 8, 8, QUERIES) * scale_s[p][None]
                t = exp_t[slot, here, :].reshape(PIECE // 8, 8, QUERIES) * scale_t[p][None]
                mix[here, :] = (s - t).reshape(PIECE, QUERIES).astype(jnp.bfloat16)
            rows = pl.ds(half * HALF, HALF)
            g = dot(mix[rows, :], q_ref[cols, :], NN)
            if block == 0:
                acc[rows, :] = g
            else:
                acc[rows, :] += g
        gq = dot(turned[HDS:], mix[...], NN) * HDS ** -0.5
        grads[:HDS, cols] = gq.astype(jnp.bfloat16)
    grads[HDS:, :] = acc[...].T.astype(jnp.bfloat16)
    fetch.wait()
    size = out_ref.shape[2]
    for d in range(out_ref.shape[0]):
        out_ref[d] = dot(grads[...], x_ref[:, d * size:(d + 1) * size], NN)


def relation_grads(head, batch, place, store, arrivals, pairs, inputs, data_ways):
    tokens, width = inputs.shape[1:]
    relays = len(arrivals) // 2
    return pl.pallas_call(
        functools.partial(relation_kernel, head, batch, relays),
        grid=(1,),
        out_shape=jax.ShapeDtypeStruct((data_ways, 2 * HDS, width // data_ways), jnp.float32),
        in_specs=[pl.BlockSpec(memory_space=pltpu.SMEM)]
        + [pl.BlockSpec(memory_space=pl.ANY)] * (1 + len(arrivals))
        + [
            pl.BlockSpec((1, tokens, 2 * HDS), lambda u: (batch, 0, head)),
            pl.BlockSpec(memory_space=pl.ANY),
        ],
        out_specs=pl.BlockSpec((data_ways, 2 * HDS, width // data_ways), lambda u: (0, 0, 0)),
        scratch_shapes=[
            pltpu.VMEM((2, tokens, HDT), jnp.bfloat16),
            pltpu.VMEM((tokens, width), jnp.bfloat16),
            pltpu.VMEM((tokens, HDS), jnp.bfloat16),
            pltpu.VMEM((tokens, HDS), jnp.bfloat16),
            pltpu.VMEM((2 * HDS, tokens), jnp.bfloat16),
            pltpu.VMEM((2, tokens, QUERIES), jnp.float32),
            pltpu.VMEM((2, tokens, QUERIES), jnp.float32),
            pltpu.VMEM((tokens, QUERIES), jnp.bfloat16),
            pltpu.VMEM((tokens, HDS), jnp.float32),
            pltpu.VMEM((2 * HDS, tokens), jnp.bfloat16),
            pltpu.SemaphoreType.DMA((3,)),
        ],
        compiler_params=pltpu.CompilerParams(vmem_limit_bytes=32 << 20),
        cost_estimate=pl.CostEstimate(flops=100_000_000, bytes_accessed=1 << 18, transcendentals=0),
    )(place, store, *arrivals, pairs, inputs)


def projection_kernel(order_ref, own_ref, far_ref, near_ref, last_ref, x_ref, out_ref, weights):
    @pl.when(pl.program_id(0) == 0)
    def _():
        size = own_ref.shape[0]
        for r, rows in enumerate((own_ref, far_ref, near_ref, last_ref)):
            weights[pl.ds(pl.multiple_of(order_ref[r] * size, size), size), :] = rows[...]

    step = 2 * HDT
    for c in range(out_ref.shape[2] // step):
        cols = pl.ds(c * step, step)
        out_ref[0, :, cols] = dot(x_ref[0], weights[:, cols], NN).astype(jnp.bfloat16)


def project(inputs, block, data):
    near = [(d, d ^ 1) for d in range(4)]
    far = [(d, d ^ 2) for d in range(4)]
    across = lax.ppermute(block, "dp", far)
    beside = lax.ppermute(block, "dp", near)
    last = lax.ppermute(across, "dp", near)
    order = jnp.stack([data, data ^ 2, data ^ 1, data ^ 3])
    batches, tokens, width = inputs.shape
    rows, cols = block.shape
    return pl.pallas_call(
        projection_kernel,
        grid=(batches,),
        out_shape=jax.ShapeDtypeStruct((batches, tokens, cols), jnp.bfloat16),
        in_specs=[
            pl.BlockSpec(memory_space=pltpu.SMEM),
            *[pl.BlockSpec((rows, cols), lambda b: (0, 0))] * 4,
            pl.BlockSpec((1, tokens, width), lambda b: (b, 0, 0)),
        ],
        out_specs=pl.BlockSpec((1, tokens, cols), lambda b: (b, 0, 0)),
        scratch_shapes=[pltpu.VMEM((width, cols), jnp.bfloat16)],
        compiler_params=pltpu.CompilerParams(vmem_limit_bytes=40 << 20),
        cost_estimate=pl.CostEstimate(flops=4_000_000_000, bytes_accessed=8 << 20, transcendentals=0),
    )(order, block, across, beside, last, inputs)


def body(teacher_panels, owner_plan, head_map, student_input, student_weights):
    model_ways = lax.axis_size("mp")
    data_ways = lax.axis_size("dp")
    groups = lax.axis_size("group")
    column = lax.axis_index("mp")
    data = lax.axis_index("dp")
    store_slots = teacher_panels.shape[0]
    tokens = teacher_panels.shape[3]
    heads = teacher_panels.shape[4] // HDT
    width = student_input.shape[-1]
    row_block = width // data_ways
    column_block = width // model_ways
    column_heads = column_block // HDS
    targets = lax.dynamic_slice_in_dim(head_map[:, 0], column * heads, heads)

    here = lax.axis_index("group")
    owner = owner_plan // store_slots
    dist = jnp.stack([(here - owner[0]) % groups, (owner[1] - here) % groups])
    slot = owner_plan % store_slots
    place = jnp.stack([dist, slot])
    ways = ([(z, (z + 1) % groups) for z in range(groups)], [(z, (z - 1) % groups) for z in range(groups)])

    def held(b, chunk):
        corner = (slot[b], 0, chunk % 2, 0, chunk // 2 * HDT)
        return lax.dynamic_slice(store, corner, (1, 1, 1, tokens, HDT))[0, 0, 0]

    store = teacher_panels
    first = [[held(b, chunk) for b in range(2)] for chunk in range(LAG)]
    first, student_weights, store = lax.optimization_barrier((first, student_weights, store))

    table = student_weights[0].reshape(2, row_block, column_heads, HDS).transpose(2, 1, 0, 3)
    table = table.reshape(1, column_heads, row_block, 2 * HDS)
    table = lax.all_to_all(jnp.broadcast_to(table, (model_ways, *table.shape[1:])), "mp", 0, 0, tiled=True)

    chunks = 2 * heads
    stages = chunks + LAG * (groups - 2)
    lead = 1 + LAG * (groups - 2)
    inputs = student_input[0, :, 0]
    arrived = []
    pairs = None
    pieces = []

    def grad(unit, place):
        head, b = divmod(unit, 2)
        sources = [arrived[2 * head + part + LAG * d][b] for d in range(groups - 1) for part in range(2)]
        return relation_grads(head, b, place, teacher_panels, sources, pairs, inputs, data_ways)

    for stage in range(stages):
        if stage < LAG:
            sends = first[stage]
        else:
            passed = arrived[stage - LAG]
            if stage == LAG:
                passed, table = lax.optimization_barrier((passed, table))
                mine = jnp.take(table.reshape(model_ways * column_heads, row_block, 2 * HDS), targets, axis=0)
                mine = mine.transpose(1, 0, 2).reshape(row_block, heads * 2 * HDS)
                pairs = project(inputs, mine, data)
            own = min(stage, chunks - 1)
            sends = [jnp.where(dist[b] == 0, held(b, own), passed[b]) for b in range(2)]
            sends, store = lax.optimization_barrier((sends, store))
        unit = stage - lead - LAG - 1
        if unit >= 0:
            piece = grad(unit, place)
            piece, sends, place = lax.optimization_barrier((piece, sends, place))
            pieces.append(piece)
        arrived.append([lax.ppermute(sends[b], "group", ways[b]) for b in range(2)])
    for unit in range(len(pieces), chunks - 1):
        pieces.append(grad(unit, place))
    reduced = [reduce_data(pieces[2 * h], pieces[2 * h + 1], data) for h in range(heads - 1)]

    names = jnp.arange(model_ways * column_heads)[:, None, None]
    slots = sum(jnp.where(targets[h] == names, reduced[h], 0.0) for h in range(heads - 1))
    slots = slots.astype(jnp.bfloat16).reshape(model_ways, column_heads, 2 * HDS, row_block)
    slots, place = lax.optimization_barrier((slots, place))
    slots = lax.all_to_all(slots, "mp", 0, 0, tiled=True)
    reduced.append(reduce_data(pieces[-1], grad(chunks - 1, place), data))
    final = jnp.broadcast_to(reduced[-1].astype(jnp.bfloat16), (model_ways, 2 * HDS, row_block))
    final = lax.all_to_all(final, "mp", 0, 0, tiled=True).astype(jnp.float32)
    goals = head_map[:, 0].reshape(model_ways, heads)[:, -1]
    result = []
    for c in range(column_heads):
        mine = (goals == column * column_heads + c)[:, None, None]
        result.append(jnp.sum(slots[:, c].astype(jnp.float32) + jnp.where(mine, final, 0.0), axis=0))
    result = jnp.stack(result).reshape(column_heads, 2, HDS, row_block)
    return result.transpose(1, 3, 0, 2).reshape(1, 2, row_block, column_block)


def reduce_data(first, second, data):
    near = [(d, d ^ 1) for d in range(4)]
    far = [(d, d ^ 2) for d in range(4)]
    first = first.reshape(2, 2, *first.shape[1:])
    second = second.reshape(2, 2, *second.shape[1:])
    core = data % 2
    chip = data // 2

    def half(which):
        return (lax.dynamic_index_in_dim(first, which, 1, keepdims=False)
                + lax.dynamic_index_in_dim(second, which, 1, keepdims=False))

    kept = half(core) + lax.ppermute(half(1 - core), "dp", near)
    got = lax.ppermute(lax.dynamic_index_in_dim(kept, 1 - chip, 0, keepdims=False), "dp", far)
    return lax.dynamic_index_in_dim(kept, chip, 0, keepdims=False) + got


def solution(mesh):
    in_specs = (
        P("group", "dp", None, None, "mp"),
        P(),
        P(),
        P("group", None, "dp", None, None),
        P("group", None, "dp", "mp"),
    )
    out_specs = P("group", None, "dp", "mp")
    return jax.shard_map(body, mesh=mesh, in_specs=in_specs, out_specs=out_specs, check_vma=False)
```

```python
import functools

import jax
import jax.numpy as jnp
from jax import lax
from jax.experimental import pallas as pl
from jax.experimental.pallas import tpu as pltpu
from jax.sharding import PartitionSpec as P

HDT = 128
HDS = 64
LOG2E = 1.4426950408889634
QUERIES = 256
HALF = 512
PIECE = 64
RELAYED = 4
LAG = 2
NT = (((1,), (1,)), ((), ()))
NN = (((1,), (0,)), ((), ()))


def dot(a, b, dims):
    return lax.dot_general(a, b, dims, preferred_element_type=jnp.float32)


def relation_kernel(head, relays, place_ref, store_ref, *refs):
    count = 2 * max(relays, 1)
    arrivals = refs[:count]
    pair_ref, x_hbm, out_ref = refs[count:count + 3]
    panel, x_ref, q_ref, k_ref, turned, turned_t, exp_s, exp_t, mix, acc, grads, sems = refs[count + 3:]
    tokens = k_ref.shape[1]

    def start(source, b, part):
        pltpu.make_async_copy(source, panel.at[b, part], sems.at[b]).start()

    for b in range(2):
        if relays:
            @pl.when(place_ref[0, b] == 0)
            def _():
                for part in range(2):
                    start(store_ref.at[place_ref[1, b], 0, part, :, pl.ds(head * HDT, HDT)], b, part)

            for d in range(relays):
                @pl.when(place_ref[0, b] == d + 1)
                def _():
                    for part in range(2):
                        start(arrivals[2 * d + part].at[b], b, part)
        else:
            for part in range(2):
                start(arrivals[b].at[part], b, part)
    fetch = pltpu.make_async_copy(x_hbm, x_ref, sems.at[2])
    fetch.start()
    blocks = tokens // QUERIES
    halves = tokens // HALF
    pieces = HALF // PIECE
    rates = (LOG2E, HDT ** -0.5 * LOG2E)

    def prepare(b):
        pair = pair_ref[b]
        q_ref[b] = pair[:, :HDS] * jnp.bfloat16(HDS ** -0.5)
        k_ref[b] = pair[:, HDS:]
        turned[b] = pair.T
        turned[b, :HDS] = turned[b, :HDS] * jnp.bfloat16(HDS ** -0.5)
        pltpu.make_async_copy(panel.at[b], panel.at[b], sems.at[b]).wait()
        turned_t[b] = panel[b, 0].T

    def exps(step, half):
        b, block = divmod(step, blocks)
        cols = pl.ds(block * QUERIES, QUERIES)
        rows = pl.ds(half * HALF, HALF)
        both = (dot(k_ref[b, rows, :], turned[b, :HDS, cols], NN), dot(panel[b, 1, rows, :], turned_t[b, :, cols], NN))
        stats = []
        for p in range(pieces):
            here = pl.ds(half * HALF + p * PIECE, PIECE)
            stat = []
            for score, rate, store in zip(both, rates, (exp_s, exp_t)):
                x = score[p * PIECE:(p + 1) * PIECE].reshape(PIECE // 8, 8, QUERIES)
                peak = jnp.max(x, axis=0)
                e = jnp.exp2((x - peak[None]) * rate)
                store[step % 2, here, :] = e.reshape(PIECE, QUERIES)
                stat.append((peak, jnp.sum(e, axis=0)))
            stats.append(stat)
        return stats

    def factors(stats):
        out = []
        for side in range(2):
            peaks = [stat[side][0] for stat in stats]
            top = peaks[0]
            for peak in peaks[1:]:
                top = jnp.maximum(top, peak)
            top = jnp.max(top, axis=0, keepdims=True)
            scale = [jnp.exp2((peak - top) * rates[side]) for peak in peaks]
            total = scale[0] * stats[0][side][1]
            for f, stat in zip(scale[1:], stats[1:]):
                total = total + f * stat[side][1]
            norm = 1.0 / jnp.sum(total, axis=0, keepdims=True)
            out.append([f * norm for f in scale])
        return out

    prepare(0)
    stats = [stat for half in range(halves) for stat in exps(0, half)]
    for step in range(2 * blocks):
        b, block = divmod(step, blocks)
        slot = step % 2
        cols = pl.ds(block * QUERIES, QUERIES)
        scale_s, scale_t = factors(stats)
        stats = []
        if step + 1 == blocks:
            prepare(1)
        for half in range(halves):
            if step + 1 < 2 * blocks:
                stats += exps(step + 1, half)
            for p in range(half * pieces, (half + 1) * pieces):
                here = pl.ds(p * PIECE, PIECE)
                s = exp_s[slot, here, :].reshape(PIECE // 8, 8, QUERIES) * scale_s[p][None]
                t = exp_t[slot, here, :].reshape(PIECE // 8, 8, QUERIES) * scale_t[p][None]
                mix[slot, here, :] = (s - t).reshape(PIECE, QUERIES).astype(jnp.bfloat16)
            rows = pl.ds(half * HALF, HALF)
            g = dot(mix[slot, rows, :], q_ref[b, cols, :], NN)
            if block == 0:
                acc[rows, :] = g
            else:
                acc[rows, :] += g
        gq = dot(turned[b, HDS:], mix[slot], NN) * HDS ** -0.5
        grads[:HDS, pl.ds(step * QUERIES, QUERIES)] = gq.astype(jnp.bfloat16)
        if block + 1 == blocks:
            grads[HDS:, pl.ds(b * tokens, tokens)] = acc[...].T.astype(jnp.bfloat16)
    fetch.wait()
    size = out_ref.shape[2]
    for d in range(out_ref.shape[0]):
        cols = pl.ds(d * size, size)
        out_ref[d] = (dot(grads[:, :tokens], x_ref[0, :, cols], NN)
                      + dot(grads[:, tokens:], x_ref[1, :, cols], NN))


def relation_grads(head, place, store, arrivals, pairs, inputs, data_ways):
    tokens, width = inputs.shape[1:]
    relays = len(arrivals) // 2 if len(arrivals) > 2 else 0
    return pl.pallas_call(
        functools.partial(relation_kernel, head, relays),
        grid=(1,),
        out_shape=jax.ShapeDtypeStruct((data_ways, 2 * HDS, width // data_ways), jnp.float32),
        in_specs=[pl.BlockSpec(memory_space=pltpu.SMEM)]
        + [pl.BlockSpec(memory_space=pl.ANY)] * (1 + len(arrivals))
        + [
            pl.BlockSpec((2, tokens, 2 * HDS), lambda u: (0, 0, head)),
            pl.BlockSpec(memory_space=pl.ANY),
        ],
        out_specs=pl.BlockSpec((data_ways, 2 * HDS, width // data_ways), lambda u: (0, 0, 0)),
        scratch_shapes=[
            pltpu.VMEM((2, 2, tokens, HDT), jnp.bfloat16),
            pltpu.VMEM((2, tokens, width), jnp.bfloat16),
            pltpu.VMEM((2, tokens, HDS), jnp.bfloat16),
            pltpu.VMEM((2, tokens, HDS), jnp.bfloat16),
            pltpu.VMEM((2, 2 * HDS, tokens), jnp.bfloat16),
            pltpu.VMEM((2, HDT, tokens), jnp.bfloat16),
            pltpu.VMEM((2, tokens, QUERIES), jnp.float32),
            pltpu.VMEM((2, tokens, QUERIES), jnp.float32),
            pltpu.VMEM((2, tokens, QUERIES), jnp.bfloat16),
            pltpu.VMEM((tokens, HDS), jnp.float32),
            pltpu.VMEM((2 * HDS, 2 * tokens), jnp.bfloat16),
            pltpu.SemaphoreType.DMA((3,)),
        ],
        compiler_params=pltpu.CompilerParams(vmem_limit_bytes=56 << 20),
        cost_estimate=pl.CostEstimate(flops=9_000_000_000, bytes_accessed=6 << 20, transcendentals=0),
    )(place, store, *arrivals, pairs, inputs)


def projection_kernel(order_ref, own_ref, far_ref, near_ref, last_ref, x_ref, out_ref, weights):
    @pl.when(pl.program_id(0) == 0)
    def _():
        size = own_ref.shape[0]
        for r, rows in enumerate((own_ref, far_ref, near_ref, last_ref)):
            weights[pl.ds(pl.multiple_of(order_ref[r] * size, size), size), :] = rows[...]

    step = 2 * HDT
    for c in range(out_ref.shape[2] // step):
        cols = pl.ds(c * step, step)
        out_ref[0, :, cols] = dot(x_ref[0], weights[:, cols], NN).astype(jnp.bfloat16)


def project(inputs, block, data):
    near = [(d, d ^ 1) for d in range(4)]
    far = [(d, d ^ 2) for d in range(4)]
    across = lax.ppermute(block, "dp", far)
    beside = lax.ppermute(block, "dp", near)
    last = lax.ppermute(across, "dp", near)
    order = jnp.stack([data, data ^ 2, data ^ 1, data ^ 3])
    batches, tokens, width = inputs.shape
    rows, cols = block.shape
    return pl.pallas_call(
        projection_kernel,
        grid=(batches,),
        out_shape=jax.ShapeDtypeStruct((batches, tokens, cols), jnp.bfloat16),
        in_specs=[
            pl.BlockSpec(memory_space=pltpu.SMEM),
            *[pl.BlockSpec((rows, cols), lambda b: (0, 0))] * 4,
            pl.BlockSpec((1, tokens, width), lambda b: (b, 0, 0)),
        ],
        out_specs=pl.BlockSpec((1, tokens, cols), lambda b: (b, 0, 0)),
        scratch_shapes=[pltpu.VMEM((width, cols), jnp.bfloat16)],
        compiler_params=pltpu.CompilerParams(vmem_limit_bytes=56 << 20),
        cost_estimate=pl.CostEstimate(flops=4_000_000_000, bytes_accessed=8 << 20, transcendentals=0),
    )(order, block, across, beside, last, inputs)


def forward_kernel(chunk, place_ref, store_ref, *refs):
    out_ref, sems = refs[-2:]
    head, part = divmod(chunk, 2)

    def held(b):
        source = store_ref.at[place_ref[1, b], 0, part, :, pl.ds(head * HDT, HDT)]
        return pltpu.make_async_copy(source, out_ref.at[b], sems.at[b])

    for b in range(2):
        if len(refs) == 2:
            held(b).start()
        else:
            @pl.when(place_ref[0, b] == 0)
            def _():
                held(b).start()

            @pl.when(place_ref[0, b] != 0)
            def _():
                pltpu.make_async_copy(refs[0].at[b], out_ref.at[b], sems.at[b]).start()

    for b in range(2):
        held(b).wait()


def forward(chunk, place, store, *arrived):
    tokens = store.shape[3]
    return pl.pallas_call(
        functools.partial(forward_kernel, chunk),
        out_shape=jax.ShapeDtypeStruct((2, tokens, HDT), store.dtype),
        in_specs=[pl.BlockSpec(memory_space=pltpu.SMEM)] + [pl.BlockSpec(memory_space=pl.ANY)] * (1 + len(arrived)),
        out_specs=pl.BlockSpec(memory_space=pltpu.VMEM),
        scratch_shapes=[pltpu.SemaphoreType.DMA((2,))],
        compiler_params=pltpu.CompilerParams(vmem_limit_bytes=56 << 20),
        cost_estimate=pl.CostEstimate(flops=0, bytes_accessed=1 << 20, transcendentals=0),
    )(place, store, *arrived)


def body(teacher_panels, owner_plan, head_map, student_input, student_weights):
    model_ways = lax.axis_size("mp")
    data_ways = lax.axis_size("dp")
    groups = lax.axis_size("group")
    column = lax.axis_index("mp")
    data = lax.axis_index("dp")
    store_slots = teacher_panels.shape[0]
    tokens = teacher_panels.shape[3]
    heads = teacher_panels.shape[4] // HDT
    width = student_input.shape[-1]
    row_block = width // data_ways
    column_block = width // model_ways
    column_heads = column_block // HDS
    targets = lax.dynamic_slice_in_dim(head_map[:, 0], column * heads, heads)

    here = lax.axis_index("group")
    owner = owner_plan // store_slots
    dist = jnp.where(data % 2 == 0, here - owner, owner - here) % groups
    slot = owner_plan % store_slots
    place = jnp.stack([dist, slot])
    ring = [(z * data_ways + d, (z + (1 if d % 2 == 0 else -1)) % groups * data_ways + d)
            for z in range(groups) for d in range(data_ways)]

    def held(b, head, count=1):
        corner = (slot[b], 0, 0, 0, head * HDT)
        return lax.dynamic_slice(store, corner, (1, 1, 2, tokens, count * HDT))[0, 0]

    store = teacher_panels
    first = [forward(chunk, place, store) for chunk in range(LAG)]
    first, student_weights, store = lax.optimization_barrier((first, student_weights, store))
    masked = [jnp.where(dist[b] == 0, held(b, head), 0) for head in range(RELAYED, heads) for b in range(2)]
    masked, place = lax.optimization_barrier((masked, place))
    masked = lax.psum(masked, "group")
    spread = [masked[2 * i:2 * i + 2] for i in range(heads - RELAYED)]

    table = student_weights[0].reshape(2, row_block, column_heads, HDS).transpose(2, 1, 0, 3)
    table = table.reshape(1, column_heads, row_block, 2 * HDS)
    table = lax.all_to_all(jnp.broadcast_to(table, (model_ways, *table.shape[1:])), "mp", 0, 0, tiled=True)

    inputs = student_input[0, :, 0]
    mine = jnp.take(table.reshape(model_ways * column_heads, row_block, 2 * HDS), targets, axis=0)
    mine = mine.transpose(1, 0, 2).reshape(row_block, heads * 2 * HDS)
    pairs = project(inputs, mine, data)
    stages = 2 * RELAYED + LAG * (groups - 2)
    lead = 2 + LAG * (groups - 2)
    arrived = []

    def grad(head, place):
        if head < RELAYED:
            sources = [arrived[2 * head + LAG * d + part] for d in range(groups - 1) for part in range(2)]
        else:
            sources = spread[head - RELAYED]
        return relation_grads(head, place, teacher_panels, sources, pairs, inputs, data_ways)

    def relay(stage, place):
        if stage < LAG:
            return first[stage]
        return forward(min(stage, 2 * RELAYED - 1), place, teacher_panels, arrived[stage - LAG])

    def send(stages, place):
        ready = [relay(stage, place) for stage in stages]
        ready, place = lax.optimization_barrier((ready, place))
        for chunk in ready:
            arrived.append(lax.ppermute(chunk, ("group", "dp"), ring))
        return place

    for stage in range(lead):
        arrived.append(lax.ppermute(relay(stage, place), ("group", "dp"), ring))
    pieces = []
    for head in range(heads - 1):
        for stage in range(lead + 2 * head, min(lead + 2 * head + 2, stages)):
            place = send([stage], place)
        piece = grad(head, place)
        piece, place = lax.optimization_barrier((piece, place))
        pieces.append(piece)

    reduced = reduce_data(jnp.stack(pieces[:RELAYED], axis=1), data)
    names = jnp.arange(model_ways * column_heads)[:, None, None]
    slots = sum(jnp.where(targets[h] == names, reduced[h], 0.0) for h in range(RELAYED))
    slots = slots.astype(jnp.bfloat16).reshape(model_ways, column_heads, 2 * HDS, row_block)
    slots, place = lax.optimization_barrier((slots, place))
    slots = lax.all_to_all(slots, "mp", 0, 0, tiled=True)
    last = reduce_data(pieces[-1][:, None], data)
    piece, slots = lax.optimization_barrier((grad(heads - 1, place), slots))
    last = jnp.concatenate([last, reduce_data(piece[:, None], data)])
    final = jnp.broadcast_to(last.astype(jnp.bfloat16), (model_ways, *last.shape))
    final = lax.all_to_all(final, "mp", 0, 0, tiled=True).astype(jnp.float32)
    goals = head_map[:, 0].reshape(model_ways, heads)[:, RELAYED:, None, None]
    result = []
    for c in range(column_heads):
        mine = goals == column * column_heads + c
        result.append(jnp.sum(slots[:, c].astype(jnp.float32), axis=0) + jnp.sum(jnp.where(mine, final, 0.0), axis=(0, 1)))
    result = jnp.stack(result).reshape(column_heads, 2, HDS, row_block)
    return result.transpose(1, 3, 0, 2).reshape(1, 2, row_block, column_block)


def reduce_data(weight, data):
    near = [(d, d ^ 1) for d in range(4)]
    far = [(d, d ^ 2) for d in range(4)]
    halves = weight.reshape(2, 2, *weight.shape[1:])
    core = data % 2
    chip = data // 2
    got = lax.ppermute(lax.dynamic_index_in_dim(halves, 1 - core, 1, keepdims=False), "dp", near)
    kept = lax.dynamic_index_in_dim(halves, core, 1, keepdims=False) + got
    got = lax.ppermute(lax.dynamic_index_in_dim(kept, 1 - chip, 0, keepdims=False), "dp", far)
    return lax.dynamic_index_in_dim(kept, chip, 0, keepdims=False) + got


def solution(mesh):
    in_specs = (
        P("group", "dp", None, None, "mp"),
        P(),
        P(),
        P("group", None, "dp", None, None),
        P("group", None, "dp", "mp"),
    )
    out_specs = P("group", None, "dp", "mp")
    return jax.shard_map(body, mesh=mesh, in_specs=in_specs, out_specs=out_specs, check_vma=False)
```

```python
import functools

import jax
import jax.numpy as jnp
from jax import lax
from jax.experimental import pallas as pl
from jax.experimental.pallas import tpu as pltpu
from jax.sharding import PartitionSpec as P

HDT = 128
HDS = 64
LOG2E = 1.4426950408889634
QUERIES = 256
HALF = 512
PIECE = 64
RELAYED = 4
ORDER = (0, 1, 4, 2, 5, 3)
NT = (((1,), (1,)), ((), ()))
NN = (((1,), (0,)), ((), ()))


def dot(a, b, dims):
    return lax.dot_general(a, b, dims, preferred_element_type=jnp.float32)


def relation_kernel(head, relays, place_ref, store_ref, *refs):
    count = max(relays, 2)
    arrivals = refs[:count]
    pair_ref, x_hbm, out_ref = refs[count:count + 3]
    (panel, x_ref, q_ref, k_ref, turned, turned_t, raw_s, raw_t, exp_s, exp_t,
     peak_s, peak_t, sum_s, sum_t, mix, acc, grads, sems) = refs[count + 3:]
    tokens = k_ref.shape[1]

    def start(source, b):
        pltpu.make_async_copy(source, panel.at[b], sems.at[b]).start()

    for b in range(2):
        if relays:
            @pl.when(place_ref[0, b] == 0)
            def _():
                start(store_ref.at[place_ref[1, b], 0, :, :, pl.ds(head * HDT, HDT)], b)

            for d in range(relays):
                @pl.when(place_ref[0, b] == d + 1)
                def _():
                    start(arrivals[d].at[b], b)
        else:
            start(arrivals[b], b)
    fetch = pltpu.make_async_copy(x_hbm, x_ref, sems.at[2])
    fetch.start()
    blocks = tokens // QUERIES
    steps = 2 * blocks
    pieces = tokens // PIECE
    rates = (LOG2E, HDT ** -0.5 * LOG2E)
    acc[...] = jnp.zeros_like(acc)
    for b in range(2):
        pair = pair_ref[b]
        q_ref[b] = pair[:, :HDS] * jnp.bfloat16(HDS ** -0.5)
        k_ref[b] = pair[:, HDS:]
        turned[b] = pair.T
        turned[b, :HDS] = turned[b, :HDS] * jnp.bfloat16(HDS ** -0.5)
    for b in range(2):
        pltpu.make_async_copy(panel.at[b], panel.at[b], sems.at[b]).wait()
        turned_t[b] = panel[b, 0].T

    def cols_of(step):
        start = step % blocks * QUERIES
        return pl.ds(start if isinstance(step, int) else pl.multiple_of(start, QUERIES), QUERIES)

    def scores(step, half):
        b, slot = step // blocks, step % 2
        rows = pl.ds(half * HALF, HALF)
        raw_s[slot, rows, :] = dot(k_ref[b, rows, :], turned[b, :HDS, cols_of(step)], NN)
        raw_t[slot, rows, :] = dot(panel[b, 1, rows, :], turned_t[b, :, cols_of(step)], NN)

    def exps(step, p):
        slot = step % 2
        rows = pl.ds(p * PIECE, PIECE)
        for raw, rate, out, peaks, sums in ((raw_s, rates[0], exp_s, peak_s, sum_s), (raw_t, rates[1], exp_t, peak_t, sum_t)):
            x = raw[slot, rows, :].reshape(PIECE // 8, 8, QUERIES)
            peak = jnp.max(x, axis=0)
            e = jnp.exp2((x - peak[None]) * rate)
            out[slot, rows, :] = e.reshape(PIECE, QUERIES)
            peaks[slot, p] = peak
            sums[slot, p] = jnp.sum(e, axis=0)

    def factors(step):
        slot = step % 2
        for rate, peaks, sums in ((rates[0], peak_s, sum_s), (rates[1], peak_t, sum_t)):
            every = peaks[slot]
            top = jnp.max(jnp.max(every, axis=0), axis=0, keepdims=True)
            scale = jnp.exp2((every - top[None]) * rate)
            norm = 1.0 / jnp.sum(jnp.sum(scale * sums[slot], axis=0), axis=0, keepdims=True)
            peaks[slot] = scale * norm[None]

    def mismatch(step, p):
        slot = step % 2
        rows = pl.ds(p * PIECE, PIECE)
        s = exp_s[slot, rows, :].reshape(PIECE // 8, 8, QUERIES) * peak_s[slot, p][None]
        t = exp_t[slot, rows, :].reshape(PIECE // 8, 8, QUERIES) * peak_t[slot, p][None]
        mix[rows, :] = (s - t).reshape(PIECE, QUERIES).astype(jnp.bfloat16)

    def gradients(step, half):
        b = step // blocks
        rows = pl.ds(half * HALF, HALF)
        acc[b, rows, :] += dot(mix[rows, :], q_ref[b, cols_of(step), :], NN)

    def finish(step):
        b = step // blocks
        gq = dot(turned[b, HDS:, :], mix[...], NN) * HDS ** -0.5
        grads[b, :HDS, cols_of(step)] = gq.astype(jnp.bfloat16)

    def iterate(new, mid, old):
        if old is not None:
            factors(old)
        for half in range(tokens // HALF):
            if new is not None:
                scores(new, half)
            for p in range(half * pieces * HALF // tokens, (half + 1) * pieces * HALF // tokens):
                if old is not None:
                    mismatch(old, p)
                if mid is not None:
                    exps(mid, p)
            if old is not None:
                gradients(old, half)
        if old is not None:
            finish(old)

    iterate(0, None, None)
    iterate(1, 0, None)

    @pl.loop(2, steps)
    def _(step):
        iterate(step, step - 1, step - 2)

    iterate(None, steps - 1, steps - 2)
    iterate(None, None, steps - 1)
    fetch.wait()
    for b in range(2):
        grads[b, HDS:, :] = acc[b].T.astype(jnp.bfloat16)
    size = out_ref.shape[2]
    for d in range(out_ref.shape[0]):
        cols = pl.ds(d * size, size)
        out_ref[d] = dot(grads[0], x_ref[0, :, cols], NN) + dot(grads[1], x_ref[1, :, cols], NN)


def relation_grads(head, place, store, arrivals, pairs, inputs, data_ways):
    tokens, width = inputs.shape[1:]
    relays = len(arrivals) if len(arrivals) > 2 else 0
    return pl.pallas_call(
        functools.partial(relation_kernel, head, relays),
        grid=(1,),
        out_shape=jax.ShapeDtypeStruct((data_ways, 2 * HDS, width // data_ways), jnp.float32),
        in_specs=[pl.BlockSpec(memory_space=pltpu.SMEM)]
        + [pl.BlockSpec(memory_space=pl.ANY)] * (1 + len(arrivals))
        + [
            pl.BlockSpec((2, tokens, 2 * HDS), lambda u: (0, 0, head)),
            pl.BlockSpec(memory_space=pl.ANY),
        ],
        out_specs=pl.BlockSpec((data_ways, 2 * HDS, width // data_ways), lambda u: (0, 0, 0)),
        scratch_shapes=[
            pltpu.VMEM((2, 2, tokens, HDT), jnp.bfloat16),
            pltpu.VMEM((2, tokens, width), jnp.bfloat16),
            pltpu.VMEM((2, tokens, HDS), jnp.bfloat16),
            pltpu.VMEM((2, tokens, HDS), jnp.bfloat16),
            pltpu.VMEM((2, 2 * HDS, tokens), jnp.bfloat16),
            pltpu.VMEM((2, HDT, tokens), jnp.bfloat16),
            *[pltpu.VMEM((2, tokens, QUERIES), jnp.float32)] * 4,
            *[pltpu.VMEM((2, tokens // PIECE, 8, QUERIES), jnp.float32)] * 4,
            pltpu.VMEM((tokens, QUERIES), jnp.bfloat16),
            pltpu.VMEM((2, tokens, HDS), jnp.float32),
            pltpu.VMEM((2, 2 * HDS, tokens), jnp.bfloat16),
            pltpu.SemaphoreType.DMA((3,)),
        ],
        compiler_params=pltpu.CompilerParams(vmem_limit_bytes=56 << 20),
        cost_estimate=pl.CostEstimate(flops=100_000_000, bytes_accessed=1 << 18, transcendentals=0),
    )(place, store, *arrivals, pairs, inputs)


def projection_kernel(order_ref, own_ref, far_ref, near_ref, last_ref, x_ref, out_ref, weights):
    @pl.when(pl.program_id(0) == 0)
    def _():
        size = own_ref.shape[0]
        for r, rows in enumerate((own_ref, far_ref, near_ref, last_ref)):
            weights[pl.ds(pl.multiple_of(order_ref[r] * size, size), size), :] = rows[...]

    step = 2 * HDT
    for c in range(out_ref.shape[2] // step):
        cols = pl.ds(c * step, step)
        out_ref[0, :, cols] = dot(x_ref[0], weights[:, cols], NN).astype(jnp.bfloat16)


def project(inputs, block, data):
    near = [(d, d ^ 1) for d in range(4)]
    far = [(d, d ^ 2) for d in range(4)]
    across = lax.ppermute(block, "dp", far)
    beside = lax.ppermute(block, "dp", near)
    last = lax.ppermute(across, "dp", near)
    order = jnp.stack([data, data ^ 2, data ^ 1, data ^ 3])
    batches, tokens, width = inputs.shape
    rows, cols = block.shape
    return pl.pallas_call(
        projection_kernel,
        grid=(batches,),
        out_shape=jax.ShapeDtypeStruct((batches, tokens, cols), jnp.bfloat16),
        in_specs=[
            pl.BlockSpec(memory_space=pltpu.SMEM),
            *[pl.BlockSpec((rows, cols), lambda b: (0, 0))] * 4,
            pl.BlockSpec((1, tokens, width), lambda b: (b, 0, 0)),
        ],
        out_specs=pl.BlockSpec((1, tokens, cols), lambda b: (b, 0, 0)),
        scratch_shapes=[pltpu.VMEM((width, cols), jnp.bfloat16)],
        compiler_params=pltpu.CompilerParams(vmem_limit_bytes=56 << 20),
        cost_estimate=pl.CostEstimate(flops=4_000_000_000, bytes_accessed=8 << 20, transcendentals=0),
    )(order, block, across, beside, last, inputs)


def body(teacher_panels, owner_plan, head_map, student_input, student_weights):
    model_ways = lax.axis_size("mp")
    data_ways = lax.axis_size("dp")
    groups = lax.axis_size("group")
    column = lax.axis_index("mp")
    data = lax.axis_index("dp")
    store_slots = teacher_panels.shape[0]
    tokens = teacher_panels.shape[3]
    heads = teacher_panels.shape[4] // HDT
    width = student_input.shape[-1]
    row_block = width // data_ways
    column_block = width // model_ways
    column_heads = column_block // HDS
    targets = lax.dynamic_slice_in_dim(head_map[:, 0], column * heads, heads)

    here = lax.axis_index("group")
    owner = owner_plan // store_slots
    dist = jnp.where(data % 2 == 0, here - owner, owner - here) % groups
    slot = owner_plan % store_slots
    place = jnp.stack([dist, slot])
    ring = [(z * data_ways + d, (z + (1 if d % 2 == 0 else -1)) % groups * data_ways + d)
            for z in range(groups) for d in range(data_ways)]
    stages = RELAYED + groups - 2
    lead = groups - 1

    def held(store, b, head):
        corner = (slot[b], 0, 0, 0, head * HDT)
        return lax.dynamic_slice(store, corner, (1, 1, 2, tokens, HDT))[0, 0]

    def both(store, head):
        return jnp.stack([held(store, b, head) for b in range(2)])

    first, store = lax.optimization_barrier((both(teacher_panels, 0), teacher_panels))
    arrived = [lax.ppermute(first, ("group", "dp"), ring)]
    masked = [jnp.where(dist[b] == 0, held(store, b, head), 0) for head in range(RELAYED, heads) for b in range(2)]
    masked, store, student_weights = lax.optimization_barrier((masked, store, student_weights))
    masked = lax.psum(masked, "group")
    spread = [masked[2 * i:2 * i + 2] for i in range(heads - RELAYED)]
    own = [both(store, head) for head in range(1, RELAYED)]
    own, got = lax.optimization_barrier((own, arrived[0]))
    arrived = [got]

    table = student_weights[0].reshape(2, row_block, column_heads, HDS).transpose(2, 1, 0, 3)
    table = table.reshape(1, column_heads, row_block, 2 * HDS)
    table = lax.all_to_all(jnp.broadcast_to(table, (model_ways, *table.shape[1:])), "mp", 0, 0, tiled=True)

    inputs = student_input[0, :, 0]
    mine = jnp.take(table.reshape(model_ways * column_heads, row_block, 2 * HDS), targets, axis=0)
    mine = mine.transpose(1, 0, 2).reshape(row_block, heads * 2 * HDS)
    pairs = project(inputs, mine, data)
    def grad(head, place):
        sources = arrived[head:head + lead] if head < RELAYED else spread[head - RELAYED]
        return relation_grads(head, place, teacher_panels, sources, pairs, inputs, data_ways)

    def relay(stage):
        mine = own[min(stage, RELAYED - 1) - 1]
        return jnp.where((dist == 0)[:, None, None, None], mine, arrived[-1])

    for stage in range(1, lead):
        arrived.append(lax.ppermute(relay(stage), ("group", "dp"), ring))
    pieces = []
    for turn, head in enumerate(ORDER):
        if head < RELAYED and head + lead < stages:
            send, place = lax.optimization_barrier((relay(head + lead), place))
            arrived.append(lax.ppermute(send, ("group", "dp"), ring))
        if turn == 1:
            spread, place = lax.optimization_barrier((spread, place))
        piece, place = lax.optimization_barrier((grad(head, place), place))
        pieces.append(piece)

    reduced = jnp.concatenate([reduce_data(jnp.stack(pieces[:-1], axis=1), data), reduce_data(pieces[-1][:, None], data)])
    names = jnp.arange(model_ways * column_heads)[:, None, None]
    slots = sum(jnp.where(targets[head] == names, reduced[turn], 0.0) for turn, head in enumerate(ORDER))
    slots = slots.astype(jnp.bfloat16).reshape(model_ways, column_heads, 2 * HDS, row_block)
    slots = lax.all_to_all(slots, "mp", 0, 0, tiled=True)
    result = jnp.sum(slots.astype(jnp.float32), axis=0).reshape(column_heads, 2, HDS, row_block)
    return result.transpose(1, 3, 0, 2).reshape(1, 2, row_block, column_block)


def reduce_data(weight, data):
    near = [(d, d ^ 1) for d in range(4)]
    far = [(d, d ^ 2) for d in range(4)]
    halves = weight.reshape(2, 2, *weight.shape[1:])
    core = data % 2
    chip = data // 2
    got = lax.ppermute(lax.dynamic_index_in_dim(halves, 1 - core, 1, keepdims=False), "dp", near)
    kept = lax.dynamic_index_in_dim(halves, core, 1, keepdims=False) + got
    got = lax.ppermute(lax.dynamic_index_in_dim(kept, 1 - chip, 0, keepdims=False), "dp", far)
    return lax.dynamic_index_in_dim(kept, chip, 0, keepdims=False) + got


def solution(mesh):
    in_specs = (
        P("group", "dp", None, None, "mp"),
        P(),
        P(),
        P("group", None, "dp", None, None),
        P("group", None, "dp", "mp"),
    )
    out_specs = P("group", None, "dp", "mp")
    return jax.shard_map(body, mesh=mesh, in_specs=in_specs, out_specs=out_specs, check_vma=False)
```

```python
import functools

import jax
import jax.numpy as jnp
from jax import lax
from jax.experimental import pallas as pl
from jax.experimental.pallas import tpu as pltpu
from jax.sharding import PartitionSpec as P

HDT = 128
HDS = 64
LOG2E = 1.4426950408889634
QUERIES = 256
HALF = 512
PIECE = 64
LAG = 2
NT = (((1,), (1,)), ((), ()))
NN = (((1,), (0,)), ((), ()))


def dot(a, b, dims):
    return lax.dot_general(a, b, dims, preferred_element_type=jnp.float32)


def relation_kernel(head, batch, relays, place_ref, store_ref, *refs):
    arrivals = refs[:2 * relays]
    pair_ref, x_hbm, out_ref = refs[2 * relays:2 * relays + 3]
    panel, x_ref, q_ref, k_ref, turned, exp_s, exp_t, mix, acc, grads, sems = refs[2 * relays + 3:]
    tokens = k_ref.shape[0]

    @pl.when(place_ref[0, batch] == 0)
    def _():
        for part in range(2):
            held = store_ref.at[place_ref[1, batch], 0, part, :, pl.ds(head * HDT, HDT)]
            pltpu.make_async_copy(held, panel.at[part], sems.at[part]).start()

    for d in range(relays):
        @pl.when(place_ref[0, batch] == d + 1)
        def _():
            for part in range(2):
                pltpu.make_async_copy(arrivals[2 * d + part].at[batch], panel.at[part], sems.at[part]).start()

    fetch = pltpu.make_async_copy(x_hbm.at[batch], x_ref, sems.at[2])
    fetch.start()
    pair = pair_ref[0]
    q_ref[...] = pair[:, :HDS] * jnp.bfloat16(HDS ** -0.5)
    k_ref[...] = pair[:, HDS:]
    turned[...] = pair.T
    turned[:HDS] = turned[:HDS] * jnp.bfloat16(HDS ** -0.5)
    for part in range(2):
        pltpu.make_async_copy(arrivals[part].at[batch], panel.at[part], sems.at[part]).wait()
    blocks = tokens // QUERIES
    halves = tokens // HALF
    pieces = HALF // PIECE
    rates = (LOG2E, HDT ** -0.5 * LOG2E)

    def exps(block, half):
        cols = pl.ds(block * QUERIES, QUERIES)
        rows = pl.ds(half * HALF, HALF)
        both = (dot(k_ref[rows, :], turned[:HDS, cols], NN), dot(panel[1, rows, :], panel[0, cols, :], NT))
        stats = []
        for p in range(pieces):
            here = pl.ds(half * HALF + p * PIECE, PIECE)
            stat = []
            for score, rate, store in zip(both, rates, (exp_s, exp_t)):
                x = score[p * PIECE:(p + 1) * PIECE].reshape(PIECE // 8, 8, QUERIES)
                peak = jnp.max(x, axis=0)
                e = jnp.exp2((x - peak[None]) * rate)
                store[block % 2, here, :] = e.reshape(PIECE, QUERIES)
                stat.append((peak, jnp.sum(e, axis=0)))
            stats.append(stat)
        return stats

    def factors(stats):
        out = []
        for side in range(2):
            peaks = [stat[side][0] for stat in stats]
            top = peaks[0]
            for peak in peaks[1:]:
                top = jnp.maximum(top, peak)
            top = jnp.max(top, axis=0, keepdims=True)
            scale = [jnp.exp2((peak - top) * rates[side]) for peak in peaks]
            total = scale[0] * stats[0][side][1]
            for f, stat in zip(scale[1:], stats[1:]):
                total = total + f * stat[side][1]
            norm = 1.0 / jnp.sum(total, axis=0, keepdims=True)
            out.append([f * norm for f in scale])
        return out

    stats = [stat for half in range(halves) for stat in exps(0, half)]
    for block in range(blocks):
        slot = block % 2
        cols = pl.ds(block * QUERIES, QUERIES)
        scale_s, scale_t = factors(stats)
        stats = []
        for half in range(halves):
            if block + 1 < blocks:
                stats += exps(block + 1, half)
            for p in range(half * pieces, (half + 1) * pieces):
                here = pl.ds(p * PIECE, PIECE)
                s = exp_s[slot, here, :].reshape(PIECE // 8, 8, QUERIES) * scale_s[p][None]
                t = exp_t[slot, here, :].reshape(PIECE // 8, 8, QUERIES) * scale_t[p][None]
                mix[here, :] = (s - t).reshape(PIECE, QUERIES).astype(jnp.bfloat16)
            rows = pl.ds(half * HALF, HALF)
            g = dot(mix[rows, :], q_ref[cols, :], NN)
            if block == 0:
                acc[rows, :] = g
            else:
                acc[rows, :] += g
        gq = dot(turned[HDS:], mix[...], NN) * HDS ** -0.5
        grads[:HDS, cols] = gq.astype(jnp.bfloat16)
    grads[HDS:, :] = acc[...].T.astype(jnp.bfloat16)
    fetch.wait()
    size = out_ref.shape[2]
    for d in range(out_ref.shape[0]):
        out_ref[d] = dot(grads[...], x_ref[:, d * size:(d + 1) * size], NN)


def relation_grads(head, batch, place, store, arrivals, pairs, inputs, data_ways):
    tokens, width = inputs.shape[1:]
    relays = len(arrivals) // 2
    return pl.pallas_call(
        functools.partial(relation_kernel, head, batch, relays),
        grid=(1,),
        out_shape=jax.ShapeDtypeStruct((data_ways, 2 * HDS, width // data_ways), jnp.float32),
        in_specs=[pl.BlockSpec(memory_space=pltpu.SMEM)]
        + [pl.BlockSpec(memory_space=pl.ANY)] * (1 + len(arrivals))
        + [
            pl.BlockSpec((1, tokens, 2 * HDS), lambda u: (batch, 0, head)),
            pl.BlockSpec(memory_space=pl.ANY),
        ],
        out_specs=pl.BlockSpec((data_ways, 2 * HDS, width // data_ways), lambda u: (0, 0, 0)),
        scratch_shapes=[
            pltpu.VMEM((2, tokens, HDT), jnp.bfloat16),
            pltpu.VMEM((tokens, width), jnp.bfloat16),
            pltpu.VMEM((tokens, HDS), jnp.bfloat16),
            pltpu.VMEM((tokens, HDS), jnp.bfloat16),
            pltpu.VMEM((2 * HDS, tokens), jnp.bfloat16),
            pltpu.VMEM((2, tokens, QUERIES), jnp.float32),
            pltpu.VMEM((2, tokens, QUERIES), jnp.float32),
            pltpu.VMEM((tokens, QUERIES), jnp.bfloat16),
            pltpu.VMEM((tokens, HDS), jnp.float32),
            pltpu.VMEM((2 * HDS, tokens), jnp.bfloat16),
            pltpu.SemaphoreType.DMA((3,)),
        ],
        compiler_params=pltpu.CompilerParams(vmem_limit_bytes=56 << 20),
        cost_estimate=pl.CostEstimate(flops=100_000_000, bytes_accessed=1 << 18, transcendentals=0),
    )(place, store, *arrivals, pairs, inputs)


def projection_kernel(order_ref, own_ref, far_ref, near_ref, last_ref, x_ref, out_ref, weights):
    @pl.when(pl.program_id(0) == 0)
    def _():
        size = own_ref.shape[0]
        for r, rows in enumerate((own_ref, far_ref, near_ref, last_ref)):
            weights[pl.ds(pl.multiple_of(order_ref[r] * size, size), size), :] = rows[...]

    step = 2 * HDT
    for c in range(out_ref.shape[2] // step):
        cols = pl.ds(c * step, step)
        out_ref[0, :, cols] = dot(x_ref[0], weights[:, cols], NN).astype(jnp.bfloat16)


def project(inputs, block, data):
    near = [(d, d ^ 1) for d in range(4)]
    far = [(d, d ^ 2) for d in range(4)]
    across = lax.ppermute(block, "dp", far)
    beside = lax.ppermute(block, "dp", near)
    last = lax.ppermute(across, "dp", near)
    order = jnp.stack([data, data ^ 2, data ^ 1, data ^ 3])
    batches, tokens, width = inputs.shape
    rows, cols = block.shape
    return pl.pallas_call(
        projection_kernel,
        grid=(batches,),
        out_shape=jax.ShapeDtypeStruct((batches, tokens, cols), jnp.bfloat16),
        in_specs=[
            pl.BlockSpec(memory_space=pltpu.SMEM),
            *[pl.BlockSpec((rows, cols), lambda b: (0, 0))] * 4,
            pl.BlockSpec((1, tokens, width), lambda b: (b, 0, 0)),
        ],
        out_specs=pl.BlockSpec((1, tokens, cols), lambda b: (b, 0, 0)),
        scratch_shapes=[pltpu.VMEM((width, cols), jnp.bfloat16)],
        compiler_params=pltpu.CompilerParams(vmem_limit_bytes=56 << 20),
        cost_estimate=pl.CostEstimate(flops=4_000_000_000, bytes_accessed=8 << 20, transcendentals=0),
    )(order, block, across, beside, last, inputs)


def body(teacher_panels, owner_plan, head_map, student_input, student_weights):
    model_ways = lax.axis_size("mp")
    data_ways = lax.axis_size("dp")
    groups = lax.axis_size("group")
    column = lax.axis_index("mp")
    data = lax.axis_index("dp")
    store_slots = teacher_panels.shape[0]
    tokens = teacher_panels.shape[3]
    heads = teacher_panels.shape[4] // HDT
    width = student_input.shape[-1]
    row_block = width // data_ways
    column_block = width // model_ways
    column_heads = column_block // HDS
    targets = lax.dynamic_slice_in_dim(head_map[:, 0], column * heads, heads)

    here = lax.axis_index("group")
    owner = owner_plan // store_slots
    dist = jnp.where(data % 2 == 0, here - owner, owner - here) % groups
    slot = owner_plan % store_slots
    place = jnp.stack([dist, slot])
    ring = [(z * data_ways + d, (z + (1 if d % 2 == 0 else -1)) % groups * data_ways + d)
            for z in range(groups) for d in range(data_ways)]

    def held(store, part, start, count):
        pick = [lax.dynamic_slice(store, (slot[b], 0, part, 0, start), (1, 1, 1, tokens, count)) for b in range(2)]
        return jnp.concatenate(pick)[:, 0, 0]

    first = [held(teacher_panels, chunk, 0, HDT) for chunk in range(LAG)]
    first, student_weights, store = lax.optimization_barrier((first, student_weights, teacher_panels))

    table = student_weights[0].reshape(2, row_block, column_heads, HDS).transpose(2, 1, 0, 3)
    table = table.reshape(1, column_heads, row_block, 2 * HDS)
    table = lax.all_to_all(jnp.broadcast_to(table, (model_ways, *table.shape[1:])), "mp", 0, 0, tiled=True)

    own = [held(store, part, HDT, (heads - 1) * HDT) for part in range(2)]
    chunks = 2 * heads
    stages = chunks + LAG * (groups - 2)
    lead = 1 + LAG * (groups - 2)
    inputs = student_input[0, :, 0]
    arrived = []
    pairs = None
    pieces = []

    def grad(unit, place):
        head, b = divmod(unit, 2)
        sources = [arrived[2 * head + part + LAG * d] for d in range(groups - 1) for part in range(2)]
        return relation_grads(head, b, place, teacher_panels, sources, pairs, inputs, data_ways)

    for stage in range(stages):
        if stage < LAG:
            send = first[stage]
        else:
            passed = arrived[stage - LAG]
            if stage == LAG:
                passed, table, own = lax.optimization_barrier((passed, table, own))
                mine = jnp.take(table.reshape(model_ways * column_heads, row_block, 2 * HDS), targets, axis=0)
                mine = mine.transpose(1, 0, 2).reshape(row_block, heads * 2 * HDS)
                pairs = project(inputs, mine, data)
            head, part = divmod(min(stage, chunks - 1), 2)
            mine = own[part][:, :, (head - 1) * HDT:head * HDT]
            send = jnp.where((dist == 0)[:, None, None], mine, passed)
            send, own = lax.optimization_barrier((send, own))
        unit = stage - lead - LAG - 1
        if unit >= 0:
            piece, send, place = lax.optimization_barrier((grad(unit, place), send, place))
            pieces.append(piece)
        arrived.append(lax.ppermute(send, ("group", "dp"), ring))
    early = heads - 2
    reduced = None
    for unit in range(len(pieces), chunks):
        if unit == 2 * early:
            reduced = reduce_data(pieces, data)
        if unit == chunks - 1:
            reduced, place = lax.optimization_barrier((reduced, place))
        piece, place = lax.optimization_barrier((grad(unit, place), place))
        pieces.append(piece)

    reduced = jnp.concatenate([reduced, reduce_data(pieces[2 * early:], data)])
    names = jnp.arange(model_ways * column_heads)[:, None, None]
    slots = sum(jnp.where(targets[h] == names, reduced[h], 0.0) for h in range(heads))
    slots = slots.astype(jnp.bfloat16).reshape(model_ways, column_heads, 2 * HDS, row_block)
    slots = lax.all_to_all(slots, "mp", 0, 0, tiled=True)
    result = jnp.sum(slots.astype(jnp.float32), axis=0).reshape(column_heads, 2, HDS, row_block)
    return result.transpose(1, 3, 0, 2).reshape(1, 2, row_block, column_block)


def reduce_data(pieces, data):
    near = [(d, d ^ 1) for d in range(4)]
    far = [(d, d ^ 2) for d in range(4)]
    core = data % 2
    chip = data // 2
    halves = [piece.reshape(2, 2, *piece.shape[1:]) for piece in pieces]

    def half(which):
        cut = [lax.dynamic_index_in_dim(piece, which, 1, keepdims=False) for piece in halves]
        return jnp.stack([cut[i] + cut[i + 1] for i in range(0, len(cut), 2)], axis=1)

    kept = half(core) + lax.ppermute(half(1 - core), "dp", near)
    got = lax.ppermute(lax.dynamic_index_in_dim(kept, 1 - chip, 0, keepdims=False), "dp", far)
    return lax.dynamic_index_in_dim(kept, chip, 0, keepdims=False) + got


def solution(mesh):
    in_specs = (
        P("group", "dp", None, None, "mp"),
        P(),
        P(),
        P("group", None, "dp", None, None),
        P("group", None, "dp", "mp"),
    )
    out_specs = P("group", None, "dp", "mp")
    return jax.shard_map(body, mesh=mesh, in_specs=in_specs, out_specs=out_specs, check_vma=False)
```

```python
import functools

import jax
import jax.numpy as jnp
from jax import lax
from jax.experimental import pallas as pl
from jax.experimental.pallas import tpu as pltpu
from jax.sharding import PartitionSpec as P

HDT = 128
HDS = 64
LOG2E = 1.4426950408889634
QUERIES = 256
HALF = 512
PIECE = 64
LAG = 2
NN = (((1,), (0,)), ((), ()))


def dot(a, b, dims):
    return lax.dot_general(a, b, dims, preferred_element_type=jnp.float32)


def relation_kernel(head, batch, relays, place_ref, store_ref, *refs):
    arrivals = refs[:2 * relays]
    pair_ref, x_hbm = refs[2 * relays:2 * relays + 2]
    refs = refs[2 * relays + 2:]
    prior = refs[:batch]
    out_ref = refs[batch]
    panel, x_ref, q_ref, k_ref, turned, turned_t, exp_s, exp_t, mix, acc, grads, sems = refs[batch + 1:]
    tokens = k_ref.shape[0]

    @pl.when(place_ref[0, batch] == 0)
    def _():
        for part in range(2):
            held = store_ref.at[place_ref[1, batch], 0, part, :, pl.ds(head * HDT, HDT)]
            pltpu.make_async_copy(held, panel.at[part], sems.at[part]).start()

    for d in range(relays):
        @pl.when(place_ref[0, batch] == d + 1)
        def _():
            for part in range(2):
                pltpu.make_async_copy(arrivals[2 * d + part].at[batch], panel.at[part], sems.at[part]).start()

    fetch = pltpu.make_async_copy(x_hbm.at[batch], x_ref, sems.at[2])
    fetch.start()
    pair = pair_ref[0]
    q_ref[...] = pair[:, :HDS] * jnp.bfloat16(HDS ** -0.5)
    k_ref[...] = pair[:, HDS:]
    turned[...] = pair.T
    turned[:HDS] = turned[:HDS] * jnp.bfloat16(HDS ** -0.5)
    for part in range(2):
        pltpu.make_async_copy(arrivals[part].at[batch], panel.at[part], sems.at[part]).wait()
    turned_t[...] = panel[0].T
    blocks = tokens // QUERIES
    halves = tokens // HALF
    pieces = HALF // PIECE
    rates = (LOG2E, HDT ** -0.5 * LOG2E)

    def exps(block, half):
        cols = pl.ds(block * QUERIES, QUERIES)
        rows = pl.ds(half * HALF, HALF)
        both = (dot(k_ref[rows, :], turned[:HDS, cols], NN), dot(panel[1, rows, :], turned_t[:, cols], NN))
        stats = []
        for p in range(pieces):
            here = pl.ds(half * HALF + p * PIECE, PIECE)
            stat = []
            for score, rate, store in zip(both, rates, (exp_s, exp_t)):
                x = score[p * PIECE:(p + 1) * PIECE].reshape(PIECE // 8, 8, QUERIES)
                peak = jnp.max(x, axis=0)
                e = jnp.exp2((x - peak[None]) * rate)
                store[block % 2, here, :] = e.reshape(PIECE, QUERIES)
                stat.append((peak, jnp.sum(e, axis=0)))
            stats.append(stat)
        return stats

    def factors(stats):
        out = []
        for side in range(2):
            peaks = [stat[side][0] for stat in stats]
            top = peaks[0]
            for peak in peaks[1:]:
                top = jnp.maximum(top, peak)
            top = jnp.max(top, axis=0, keepdims=True)
            scale = [jnp.exp2((peak - top) * rates[side]) for peak in peaks]
            total = scale[0] * stats[0][side][1]
            for f, stat in zip(scale[1:], stats[1:]):
                total = total + f * stat[side][1]
            norm = 1.0 / jnp.sum(total, axis=0, keepdims=True)
            out.append([f * norm for f in scale])
        return out

    stats = [stat for half in range(halves) for stat in exps(0, half)]
    for block in range(blocks):
        slot = block % 2
        cols = pl.ds(block * QUERIES, QUERIES)
        scale_s, scale_t = factors(stats)
        stats = []
        for half in range(halves):
            if block + 1 < blocks:
                stats += exps(block + 1, half)
            for p in range(half * pieces, (half + 1) * pieces):
                here = pl.ds(p * PIECE, PIECE)
                s = exp_s[slot, here, :].reshape(PIECE // 8, 8, QUERIES) * scale_s[p][None]
                t = exp_t[slot, here, :].reshape(PIECE // 8, 8, QUERIES) * scale_t[p][None]
                mix[here, :] = (s - t).reshape(PIECE, QUERIES).astype(jnp.bfloat16)
            rows = pl.ds(half * HALF, HALF)
            g = dot(mix[rows, :], q_ref[cols, :], NN)
            if block == 0:
                acc[rows, :] = g
            else:
                acc[rows, :] += g
        gq = dot(turned[HDS:], mix[...], NN) * HDS ** -0.5
        grads[:HDS, cols] = gq.astype(jnp.bfloat16)
    grads[HDS:, :] = acc[...].T.astype(jnp.bfloat16)
    fetch.wait()
    size = out_ref.shape[2]
    for d in range(out_ref.shape[0]):
        weight = dot(grads[...], x_ref[:, d * size:(d + 1) * size], NN)
        out_ref[d] = prior[0][d] + weight if batch else weight


def relation_grads(head, batch, place, store, arrivals, pairs, inputs, prior, data_ways):
    tokens, width = inputs.shape[1:]
    relays = len(arrivals) // 2
    return pl.pallas_call(
        functools.partial(relation_kernel, head, batch, relays),
        grid=(1,),
        out_shape=jax.ShapeDtypeStruct((data_ways, 2 * HDS, width // data_ways), jnp.float32),
        in_specs=[pl.BlockSpec(memory_space=pltpu.SMEM)]
        + [pl.BlockSpec(memory_space=pl.ANY)] * (1 + len(arrivals))
        + [
            pl.BlockSpec((1, tokens, 2 * HDS), lambda u: (batch, 0, head)),
            pl.BlockSpec(memory_space=pl.ANY),
        ]
        + [pl.BlockSpec((data_ways, 2 * HDS, width // data_ways), lambda u: (0, 0, 0))] * len(prior),
        out_specs=pl.BlockSpec((data_ways, 2 * HDS, width // data_ways), lambda u: (0, 0, 0)),
        scratch_shapes=[
            pltpu.VMEM((2, tokens, HDT), jnp.bfloat16),
            pltpu.VMEM((tokens, width), jnp.bfloat16),
            pltpu.VMEM((tokens, HDS), jnp.bfloat16),
            pltpu.VMEM((tokens, HDS), jnp.bfloat16),
            pltpu.VMEM((2 * HDS, tokens), jnp.bfloat16),
            pltpu.VMEM((HDT, tokens), jnp.bfloat16),
            pltpu.VMEM((2, tokens, QUERIES), jnp.float32),
            pltpu.VMEM((2, tokens, QUERIES), jnp.float32),
            pltpu.VMEM((tokens, QUERIES), jnp.bfloat16),
            pltpu.VMEM((tokens, HDS), jnp.float32),
            pltpu.VMEM((2 * HDS, tokens), jnp.bfloat16),
            pltpu.SemaphoreType.DMA((3,)),
        ],
        compiler_params=pltpu.CompilerParams(vmem_limit_bytes=24 << 20),
        cost_estimate=pl.CostEstimate(flops=100_000_000, bytes_accessed=1 << 18, transcendentals=0),
    )(place, store, *arrivals, pairs, inputs, *prior)


def projection_kernel(order_ref, own_ref, far_ref, near_ref, last_ref, x_ref, out_ref, weights):
    @pl.when(pl.program_id(0) == 0)
    def _():
        size = own_ref.shape[0]
        for r, rows in enumerate((own_ref, far_ref, near_ref, last_ref)):
            weights[pl.ds(pl.multiple_of(order_ref[r] * size, size), size), :] = rows[...]

    step = 2 * HDT
    for c in range(out_ref.shape[2] // step):
        cols = pl.ds(c * step, step)
        out_ref[0, :, cols] = dot(x_ref[0], weights[:, cols], NN).astype(jnp.bfloat16)


def pick_kernel(targets_ref, table_ref, out_ref):
    out_ref[...] = table_ref[0]


def pick(table, targets):
    rows, cols = table.shape[1:]
    count = targets.shape[0]
    return pl.pallas_call(
        pick_kernel,
        grid_spec=pltpu.PrefetchScalarGridSpec(
            num_scalar_prefetch=1,
            grid=(count,),
            in_specs=[pl.BlockSpec((1, rows, cols), lambda h, targets: (targets[h], 0, 0))],
            out_specs=pl.BlockSpec((rows, cols), lambda h, targets: (0, h)),
        ),
        out_shape=jax.ShapeDtypeStruct((rows, count * cols), table.dtype),
        cost_estimate=pl.CostEstimate(flops=0, bytes_accessed=1 << 20, transcendentals=0),
    )(targets, table)


def project(inputs, block, data):
    near = [(d, d ^ 1) for d in range(4)]
    far = [(d, d ^ 2) for d in range(4)]
    across = lax.ppermute(block, "dp", far)
    beside = lax.ppermute(block, "dp", near)
    last = lax.ppermute(across, "dp", near)
    order = jnp.stack([data, data ^ 2, data ^ 1, data ^ 3])
    batches, tokens, width = inputs.shape
    rows, cols = block.shape
    return pl.pallas_call(
        projection_kernel,
        grid=(batches,),
        out_shape=jax.ShapeDtypeStruct((batches, tokens, cols), jnp.bfloat16),
        in_specs=[
            pl.BlockSpec(memory_space=pltpu.SMEM),
            *[pl.BlockSpec((rows, cols), lambda b: (0, 0))] * 4,
            pl.BlockSpec((1, tokens, width), lambda b: (b, 0, 0)),
        ],
        out_specs=pl.BlockSpec((1, tokens, cols), lambda b: (b, 0, 0)),
        scratch_shapes=[pltpu.VMEM((width, cols), jnp.bfloat16)],
        compiler_params=pltpu.CompilerParams(vmem_limit_bytes=24 << 20),
        cost_estimate=pl.CostEstimate(flops=4_000_000_000, bytes_accessed=8 << 20, transcendentals=0),
    )(order, block, across, beside, last, inputs)


def body(teacher_panels, owner_plan, head_map, student_input, student_weights):
    model_ways = lax.axis_size("mp")
    data_ways = lax.axis_size("dp")
    groups = lax.axis_size("group")
    column = lax.axis_index("mp")
    data = lax.axis_index("dp")
    store_slots = teacher_panels.shape[0]
    tokens = teacher_panels.shape[3]
    heads = teacher_panels.shape[4] // HDT
    width = student_input.shape[-1]
    row_block = width // data_ways
    column_block = width // model_ways
    column_heads = column_block // HDS
    targets = lax.dynamic_slice_in_dim(head_map[:, 0], column * heads, heads)

    here = lax.axis_index("group")
    owner = owner_plan // store_slots
    dist = jnp.where(data % 2 == 0, here - owner, owner - here) % groups
    slot = owner_plan % store_slots
    place = jnp.stack([dist, slot])
    ring = [(z * data_ways + d, (z + (1 if d % 2 == 0 else -1)) % groups * data_ways + d)
            for z in range(groups) for d in range(data_ways)]

    def held(store, part, start, count):
        pick = [lax.dynamic_slice(store, (slot[b], 0, part, 0, start), (1, 1, 1, tokens, count)) for b in range(2)]
        return jnp.concatenate(pick)[:, 0, 0]

    first = [held(teacher_panels, chunk, 0, HDT) for chunk in range(LAG)]
    first, student_weights, store = lax.optimization_barrier((first, student_weights, teacher_panels))

    table = student_weights[0].reshape(2, row_block, column_heads, HDS).transpose(2, 1, 0, 3)
    table = table.reshape(1, column_heads, row_block, 2 * HDS)
    table = lax.all_to_all(jnp.broadcast_to(table, (model_ways, *table.shape[1:])), "mp", 0, 0, tiled=True)

    own = [held(store, part, HDT, (heads - 1) * HDT) for part in range(2)]
    chunks = 2 * heads
    stages = chunks + LAG * (groups - 2)
    lead = 1 + LAG * (groups - 2)
    inputs = student_input[0, :, 0]
    arrived = []
    pairs = None
    pieces = []

    def grad(unit, place):
        head, b = divmod(unit, 2)
        sources = [arrived[2 * head + part + LAG * d] for d in range(groups - 1) for part in range(2)]
        return relation_grads(head, b, place, teacher_panels, sources, pairs, inputs, pieces[-1:] * b, data_ways)

    for stage in range(stages):
        if stage < LAG:
            send = first[stage]
        else:
            passed = arrived[stage - LAG]
            if stage == LAG:
                passed, table, own = lax.optimization_barrier((passed, table, own))
                mine = pick(table.reshape(model_ways * column_heads, row_block, 2 * HDS), targets)
                pairs = project(inputs, mine, data)
            head, part = divmod(min(stage, chunks - 1), 2)
            mine = own[part][:, :, (head - 1) * HDT:head * HDT]
            send = jnp.where((dist == 0)[:, None, None], mine, passed)
            send, own = lax.optimization_barrier((send, own))
        unit = stage - lead - LAG - 1
        if unit >= 0:
            piece, send, place = lax.optimization_barrier((grad(unit, place), send, place))
            pieces.append(piece)
        arrived.append(lax.ppermute(send, ("group", "dp"), ring))
    early = heads - 2
    reduced = None
    for unit in range(len(pieces), chunks):
        if unit == 2 * early:
            reduced = reduce_data(pieces[1::2], data)
        if unit == chunks - 1:
            reduced, place = lax.optimization_barrier((reduced, place))
        piece, place = lax.optimization_barrier((grad(unit, place), place))
        pieces.append(piece)

    reduced = jnp.concatenate([reduced, reduce_data(pieces[2 * early + 1::2], data)])
    names = jnp.arange(model_ways * column_heads)[:, None, None]
    slots = sum(jnp.where(targets[h] == names, reduced[h], 0.0) for h in range(heads))
    slots = slots.astype(jnp.bfloat16).reshape(model_ways, column_heads, 2 * HDS, row_block)
    slots = lax.all_to_all(slots, "mp", 0, 0, tiled=True)
    result = jnp.sum(slots.astype(jnp.float32), axis=0).reshape(column_heads, 2, HDS, row_block)
    return result.transpose(1, 3, 0, 2).reshape(1, 2, row_block, column_block)


def reduce_data(pieces, data):
    near = [(d, d ^ 1) for d in range(4)]
    far = [(d, d ^ 2) for d in range(4)]
    core = data % 2
    chip = data // 2
    halves = [piece.reshape(2, 2, *piece.shape[1:]) for piece in pieces]

    def half(which):
        return jnp.stack([lax.dynamic_index_in_dim(piece, which, 1, keepdims=False) for piece in halves], axis=1)

    kept = half(core) + lax.ppermute(half(1 - core), "dp", near)
    got = lax.ppermute(lax.dynamic_index_in_dim(kept, 1 - chip, 0, keepdims=False), "dp", far)
    return lax.dynamic_index_in_dim(kept, chip, 0, keepdims=False) + got


def solution(mesh):
    in_specs = (
        P("group", "dp", None, None, "mp"),
        P(),
        P(),
        P("group", None, "dp", None, None),
        P("group", None, "dp", "mp"),
    )
    out_specs = P("group", None, "dp", "mp")
    return jax.shard_map(body, mesh=mesh, in_specs=in_specs, out_specs=out_specs, check_vma=False)
```

```python
import functools

import jax
import jax.numpy as jnp
from jax import lax
from jax.experimental import pallas as pl
from jax.experimental.pallas import tpu as pltpu
from jax.sharding import PartitionSpec as P

HDT = 128
HDS = 64
LOG2E = 1.4426950408889634
QUERIES = 256
HALF = 512
PIECE = 64
LAG = 2
NN = (((1,), (0,)), ((), ()))


def dot(a, b, dims):
    return lax.dot_general(a, b, dims, preferred_element_type=jnp.float32)


def relation_kernel(head, batch, relays, place_ref, store_ref, *refs):
    arrivals = refs[:2 * relays]
    pair_hbm, x_hbm = refs[2 * relays:2 * relays + 2]
    refs = refs[2 * relays + 2:]
    prior = refs[:batch]
    out_ref = refs[batch]
    panel, x_ref, pair_ref, prior_ref, q_ref, k_ref, turned, turned_t, exp_s, exp_t, mix, acc, grads, sems = refs[batch + 1:]
    tokens = k_ref.shape[0]

    @pl.when(place_ref[0, batch] == 0)
    def _():
        for part in range(2):
            held = store_ref.at[place_ref[1, batch], 0, part, :, pl.ds(head * HDT, HDT)]
            pltpu.make_async_copy(held, panel.at[part], sems.at[part]).start()

    for d in range(relays):
        @pl.when(place_ref[0, batch] == d + 1)
        def _():
            for part in range(2):
                pltpu.make_async_copy(arrivals[2 * d + part].at[batch], panel.at[part], sems.at[part]).start()

    load = pltpu.make_async_copy(pair_hbm.at[batch, head], pair_ref, sems.at[3])
    load.start()
    fetch = pltpu.make_async_copy(x_hbm.at[batch], x_ref, sems.at[2])
    fetch.start()
    for ref in prior:
        pltpu.make_async_copy(ref, prior_ref, sems.at[4]).start()
    load.wait()
    pair = pair_ref[...]
    q_ref[...] = pair[:, :HDS] * jnp.bfloat16(HDS ** -0.5)
    k_ref[...] = pair[:, HDS:]
    turned[...] = pair.T
    turned[:HDS] = turned[:HDS] * jnp.bfloat16(HDS ** -0.5)
    for part in range(2):
        pltpu.make_async_copy(arrivals[part].at[batch], panel.at[part], sems.at[part]).wait()
    turned_t[...] = panel[0].T
    blocks = tokens // QUERIES
    halves = tokens // HALF
    pieces = HALF // PIECE
    rates = (LOG2E, HDT ** -0.5 * LOG2E)

    def exps(block, half):
        cols = pl.ds(block * QUERIES, QUERIES)
        rows = pl.ds(half * HALF, HALF)
        both = (dot(k_ref[rows, :], turned[:HDS, cols], NN), dot(panel[1, rows, :], turned_t[:, cols], NN))
        stats = []
        for p in range(pieces):
            here = pl.ds(half * HALF + p * PIECE, PIECE)
            stat = []
            for score, rate, store in zip(both, rates, (exp_s, exp_t)):
                x = score[p * PIECE:(p + 1) * PIECE].reshape(PIECE // 8, 8, QUERIES)
                peak = jnp.max(x, axis=0)
                e = jnp.exp2((x - peak[None]) * rate)
                store[block % 2, here, :] = e.reshape(PIECE, QUERIES)
                stat.append((peak, jnp.sum(e, axis=0)))
            stats.append(stat)
        return stats

    def factors(stats):
        out = []
        for side in range(2):
            peaks = [stat[side][0] for stat in stats]
            top = peaks[0]
            for peak in peaks[1:]:
                top = jnp.maximum(top, peak)
            top = jnp.max(top, axis=0, keepdims=True)
            scale = [jnp.exp2((peak - top) * rates[side]) for peak in peaks]
            total = scale[0] * stats[0][side][1]
            for f, stat in zip(scale[1:], stats[1:]):
                total = total + f * stat[side][1]
            norm = 1.0 / jnp.sum(total, axis=0, keepdims=True)
            out.append([f * norm for f in scale])
        return out

    stats = [stat for half in range(halves) for stat in exps(0, half)]
    for block in range(blocks):
        slot = block % 2
        cols = pl.ds(block * QUERIES, QUERIES)
        scale_s, scale_t = factors(stats)
        stats = []
        for half in range(halves):
            if block + 1 < blocks:
                stats += exps(block + 1, half)
            for p in range(half * pieces, (half + 1) * pieces):
                here = pl.ds(p * PIECE, PIECE)
                s = exp_s[slot, here, :].reshape(PIECE // 8, 8, QUERIES) * scale_s[p][None]
                t = exp_t[slot, here, :].reshape(PIECE // 8, 8, QUERIES) * scale_t[p][None]
                mix[here, :] = (s - t).reshape(PIECE, QUERIES).astype(jnp.bfloat16)
            rows = pl.ds(half * HALF, HALF)
            g = dot(mix[rows, :], q_ref[cols, :], NN)
            if block == 0:
                acc[rows, :] = g
            else:
                acc[rows, :] += g
        gq = dot(turned[HDS:], mix[...], NN) * HDS ** -0.5
        grads[:HDS, cols] = gq.astype(jnp.bfloat16)
    grads[HDS:, :] = acc[...].T.astype(jnp.bfloat16)
    fetch.wait()
    for ref in prior:
        pltpu.make_async_copy(ref, prior_ref, sems.at[4]).wait()
    size = out_ref.shape[2]
    for d in range(out_ref.shape[0]):
        weight = dot(grads[...], x_ref[:, d * size:(d + 1) * size], NN)
        out_ref[d] = prior_ref[d] + weight if batch else weight


def relation_grads(head, batch, place, store, arrivals, pairs, inputs, prior, data_ways):
    tokens, width = inputs.shape[1:]
    relays = len(arrivals) // 2
    return pl.pallas_call(
        functools.partial(relation_kernel, head, batch, relays),
        grid=(1,),
        out_shape=jax.ShapeDtypeStruct((data_ways, 2 * HDS, width // data_ways), jnp.float32),
        in_specs=[pl.BlockSpec(memory_space=pltpu.SMEM)]
        + [pl.BlockSpec(memory_space=pl.ANY)] * (3 + len(arrivals) + len(prior)),
        out_specs=pl.BlockSpec((data_ways, 2 * HDS, width // data_ways), lambda u: (0, 0, 0)),
        scratch_shapes=[
            pltpu.VMEM((2, tokens, HDT), jnp.bfloat16),
            pltpu.VMEM((tokens, width), jnp.bfloat16),
            pltpu.VMEM((tokens, 2 * HDS), jnp.bfloat16),
            pltpu.VMEM((data_ways, 2 * HDS, width // data_ways), jnp.float32),
            pltpu.VMEM((tokens, HDS), jnp.bfloat16),
            pltpu.VMEM((tokens, HDS), jnp.bfloat16),
            pltpu.VMEM((2 * HDS, tokens), jnp.bfloat16),
            pltpu.VMEM((HDT, tokens), jnp.bfloat16),
            pltpu.VMEM((2, tokens, QUERIES), jnp.float32),
            pltpu.VMEM((2, tokens, QUERIES), jnp.float32),
            pltpu.VMEM((tokens, QUERIES), jnp.bfloat16),
            pltpu.VMEM((tokens, HDS), jnp.float32),
            pltpu.VMEM((2 * HDS, tokens), jnp.bfloat16),
            pltpu.SemaphoreType.DMA((5,)),
        ],
        compiler_params=pltpu.CompilerParams(vmem_limit_bytes=56 << 20),
        cost_estimate=pl.CostEstimate(flops=100_000_000, bytes_accessed=1 << 18, transcendentals=0),
    )(place, store, *arrivals, pairs, inputs, *prior)


def projection_kernel(order_ref, own_ref, far_ref, near_ref, last_ref, x_ref, out_ref, weights):
    @pl.when(pl.program_id(0) == 0)
    def _():
        size = own_ref.shape[0]
        for r, rows in enumerate((own_ref, far_ref, near_ref, last_ref)):
            weights[pl.ds(pl.multiple_of(order_ref[r] * size, size), size), :] = rows[...]

    for c in range(out_ref.shape[1] // 2):
        pair = dot(x_ref[0], weights[:, 4 * c * HDS:4 * (c + 1) * HDS], NN).astype(jnp.bfloat16)
        out_ref[0, 2 * c] = pair[:, :2 * HDS]
        out_ref[0, 2 * c + 1] = pair[:, 2 * HDS:]


def pick_kernel(targets_ref, table_ref, out_ref, sem):
    cols = table_ref.shape[2]
    copies = [pltpu.make_async_copy(table_ref.at[targets_ref[h]], out_ref.at[:, pl.ds(h * cols, cols)], sem.at[h])
              for h in range(out_ref.shape[1] // cols)]
    for copy in copies:
        copy.start()
    for copy in copies:
        copy.wait()


def pick(table, targets):
    rows, cols = table.shape[1:]
    count = targets.shape[0]
    return pl.pallas_call(
        pick_kernel,
        in_specs=[pl.BlockSpec(memory_space=pltpu.SMEM), pl.BlockSpec(memory_space=pl.ANY)],
        out_specs=pl.BlockSpec(memory_space=pltpu.VMEM),
        out_shape=jax.ShapeDtypeStruct((rows, count * cols), table.dtype),
        scratch_shapes=[pltpu.SemaphoreType.DMA((count,))],
        cost_estimate=pl.CostEstimate(flops=0, bytes_accessed=1 << 20, transcendentals=0),
    )(targets, table)


def slots_kernel(targets_ref, first_ref, last_ref, out_ref):
    parts = [ref.at[h] for ref in (first_ref, last_ref) for h in range(ref.shape[0])]
    for s in range(out_ref.shape[0]):
        total = jnp.where(targets_ref[0] == s, parts[0][...], 0.0)
        for h in range(1, len(parts)):
            total = total + jnp.where(targets_ref[h] == s, parts[h][...], 0.0)
        out_ref[s] = total.astype(out_ref.dtype)


def add_slots(targets, first, last, count):
    return pl.pallas_call(
        slots_kernel,
        in_specs=[pl.BlockSpec(memory_space=pltpu.SMEM)] + [pl.BlockSpec(memory_space=pltpu.VMEM)] * 2,
        out_specs=pl.BlockSpec(memory_space=pltpu.VMEM),
        out_shape=jax.ShapeDtypeStruct((count, *first.shape[1:]), jnp.bfloat16),
        cost_estimate=pl.CostEstimate(flops=0, bytes_accessed=1 << 20, transcendentals=0),
    )(targets, first, last)


def project(inputs, block, data):
    near = [(d, d ^ 1) for d in range(4)]
    far = [(d, d ^ 2) for d in range(4)]
    across = lax.ppermute(block, "dp", far)
    beside = lax.ppermute(block, "dp", near)
    last = lax.ppermute(across, "dp", near)
    order = jnp.stack([data, data ^ 2, data ^ 1, data ^ 3])
    batches, tokens, width = inputs.shape
    rows, cols = block.shape
    return pl.pallas_call(
        projection_kernel,
        grid=(batches,),
        out_shape=jax.ShapeDtypeStruct((batches, cols // (2 * HDS), tokens, 2 * HDS), jnp.bfloat16),
        in_specs=[
            pl.BlockSpec(memory_space=pltpu.SMEM),
            *[pl.BlockSpec((rows, cols), lambda b: (0, 0))] * 4,
            pl.BlockSpec((1, tokens, width), lambda b: (b, 0, 0)),
        ],
        out_specs=pl.BlockSpec((1, cols // (2 * HDS), tokens, 2 * HDS), lambda b: (b, 0, 0, 0)),
        scratch_shapes=[pltpu.VMEM((width, cols), jnp.bfloat16)],
        compiler_params=pltpu.CompilerParams(vmem_limit_bytes=56 << 20),
        cost_estimate=pl.CostEstimate(flops=4_000_000_000, bytes_accessed=8 << 20, transcendentals=0),
    )(order, block, across, beside, last, inputs)


def body(teacher_panels, owner_plan, head_map, student_input, student_weights):
    model_ways = lax.axis_size("mp")
    data_ways = lax.axis_size("dp")
    groups = lax.axis_size("group")
    column = lax.axis_index("mp")
    data = lax.axis_index("dp")
    store_slots = teacher_panels.shape[0]
    tokens = teacher_panels.shape[3]
    heads = teacher_panels.shape[4] // HDT
    width = student_input.shape[-1]
    row_block = width // data_ways
    column_block = width // model_ways
    column_heads = column_block // HDS
    targets = lax.dynamic_slice_in_dim(head_map[:, 0], column * heads, heads)

    here = lax.axis_index("group")
    owner = owner_plan // store_slots
    dist = jnp.where(data % 2 == 0, here - owner, owner - here) % groups
    slot = owner_plan % store_slots
    place = jnp.stack([dist, slot])
    ring = [(z * data_ways + d, (z + (1 if d % 2 == 0 else -1)) % groups * data_ways + d)
            for z in range(groups) for d in range(data_ways)]

    def held(store, part, start, count):
        pick = [lax.dynamic_slice(store, (slot[b], 0, part, 0, start), (1, 1, 1, tokens, count)) for b in range(2)]
        return jnp.concatenate(pick)[:, 0, 0]

    first = [held(teacher_panels, chunk, 0, HDT) for chunk in range(LAG)]
    first, student_weights, store = lax.optimization_barrier((first, student_weights, teacher_panels))

    table = student_weights[0].reshape(2, row_block, column_heads, HDS).transpose(2, 1, 0, 3)
    table = table.reshape(1, column_heads, row_block, 2 * HDS)
    table = lax.all_to_all(jnp.broadcast_to(table, (model_ways, *table.shape[1:])), "mp", 0, 0, tiled=True)

    own = [held(store, part, HDT, (heads - 1) * HDT) for part in range(2)]
    chunks = 2 * heads
    stages = chunks + LAG * (groups - 2)
    lead = 1 + LAG * (groups - 2)
    inputs = student_input[0, :, 0]
    arrived = []
    pairs = None
    pieces = []

    def grad(unit, place):
        head, b = divmod(unit, 2)
        sources = [arrived[2 * head + part + LAG * d] for d in range(groups - 1) for part in range(2)]
        return relation_grads(head, b, place, teacher_panels, sources, pairs, inputs, pieces[-1:] * b, data_ways)

    for stage in range(stages):
        if stage < LAG:
            send = first[stage]
        else:
            passed = arrived[stage - LAG]
            if stage == LAG + 1:
                passed, table, own = lax.optimization_barrier((passed, table, own))
                mine = pick(table.reshape(model_ways * column_heads, row_block, 2 * HDS), targets)
                pairs = project(inputs, mine, data)
            head, part = divmod(min(stage, chunks - 1), 2)
            mine = own[part][:, :, (head - 1) * HDT:head * HDT]
            send = jnp.where((dist == 0)[:, None, None], mine, passed)
            send, own = lax.optimization_barrier((send, own))
        unit = stage - lead - LAG - 1
        if unit >= 0:
            piece, send, place = lax.optimization_barrier((grad(unit, place), send, place))
            pieces.append(piece)
        arrived.append(lax.ppermute(send, ("group", "dp"), ring))
    early = heads - 2
    reduced = None
    for unit in range(len(pieces), chunks):
        if unit == 2 * early:
            reduced = reduce_data(pieces[1::2], data)
        if unit == chunks - 1:
            reduced, place = lax.optimization_barrier((reduced, place))
        piece, place = lax.optimization_barrier((grad(unit, place), place))
        pieces.append(piece)

    slots = add_slots(targets, reduced, reduce_data(pieces[2 * early + 1::2], data), model_ways * column_heads)
    slots = slots.reshape(model_ways, column_heads, 2 * HDS, row_block)
    slots = lax.all_to_all(slots, "mp", 0, 0, tiled=True)
    result = jnp.sum(slots.astype(jnp.float32), axis=0).reshape(column_heads, 2, HDS, row_block)
    return result.transpose(1, 3, 0, 2).reshape(1, 2, row_block, column_block)


def reduce_data(pieces, data):
    near = [(d, d ^ 1) for d in range(4)]
    far = [(d, d ^ 2) for d in range(4)]
    core = data % 2
    chip = data // 2
    halves = [piece.reshape(2, 2, *piece.shape[1:]) for piece in pieces]

    def half(which):
        return jnp.stack([lax.dynamic_index_in_dim(piece, which, 1, keepdims=False) for piece in halves], axis=1)

    kept = half(core) + lax.ppermute(half(1 - core), "dp", near)
    got = lax.ppermute(lax.dynamic_index_in_dim(kept, 1 - chip, 0, keepdims=False), "dp", far)
    return lax.dynamic_index_in_dim(kept, chip, 0, keepdims=False) + got


def solution(mesh):
    in_specs = (
        P("group", "dp", None, None, "mp"),
        P(),
        P(),
        P("group", None, "dp", None, None),
        P("group", None, "dp", "mp"),
    )
    out_specs = P("group", None, "dp", "mp")
    return jax.shard_map(body, mesh=mesh, in_specs=in_specs, out_specs=out_specs, check_vma=False)
```

```python
import functools

import jax
import jax.numpy as jnp
from jax import lax
from jax.experimental import pallas as pl
from jax.experimental.pallas import tpu as pltpu
from jax.sharding import PartitionSpec as P

HDT = 128
HDS = 64
LOG2E = 1.4426950408889634
QUERIES = 256
HALF = 512
PIECE = 64
LAG = 2
NN = (((1,), (0,)), ((), ()))


def dot(a, b, dims):
    return lax.dot_general(a, b, dims, preferred_element_type=jnp.float32)


def relation_kernel(head, batch, relays, place_ref, store_ref, *refs):
    arrivals = refs[:2 * relays]
    pair_hbm, x_hbm = refs[2 * relays:2 * relays + 2]
    refs = refs[2 * relays + 2:]
    prior = refs[:batch]
    out_ref = refs[batch]
    panel, x_ref, pair_ref, prior_ref, q_ref, k_ref, turned, turned_t, exp_s, exp_t, mix, acc, grads, sems = refs[batch + 1:]
    tokens = k_ref.shape[0]

    @pl.when(place_ref[0, batch] == 0)
    def _():
        for part in range(2):
            held = store_ref.at[place_ref[1, batch], 0, part, :, pl.ds(head * HDT, HDT)]
            pltpu.make_async_copy(held, panel.at[part], sems.at[part]).start()

    for d in range(relays):
        @pl.when(place_ref[0, batch] == d + 1)
        def _():
            for part in range(2):
                pltpu.make_async_copy(arrivals[2 * d + part].at[batch], panel.at[part], sems.at[part]).start()

    load = pltpu.make_async_copy(pair_hbm.at[batch, head], pair_ref, sems.at[3])
    load.start()
    load.wait()
    pair = pair_ref[...]
    q_ref[...] = pair[:, :HDS] * jnp.bfloat16(HDS ** -0.5)
    k_ref[...] = pair[:, HDS:]
    turned[...] = pair.T
    turned[:HDS] = turned[:HDS] * jnp.bfloat16(HDS ** -0.5)
    for part in range(2):
        pltpu.make_async_copy(arrivals[part].at[batch], panel.at[part], sems.at[part]).wait()
    fetch = pltpu.make_async_copy(x_hbm.at[batch], x_ref, sems.at[2])
    fetch.start()
    for ref in prior:
        pltpu.make_async_copy(ref, prior_ref, sems.at[4]).start()
    turned_t[...] = panel[0].T
    blocks = tokens // QUERIES
    halves = tokens // HALF
    pieces = HALF // PIECE
    rates = (LOG2E, HDT ** -0.5 * LOG2E)

    def exps(block, half):
        cols = pl.ds(block * QUERIES, QUERIES)
        rows = pl.ds(half * HALF, HALF)
        both = (dot(k_ref[rows, :], turned[:HDS, cols], NN), dot(panel[1, rows, :], turned_t[:, cols], NN))
        stats = []
        for p in range(pieces):
            here = pl.ds(half * HALF + p * PIECE, PIECE)
            stat = []
            for score, rate, store in zip(both, rates, (exp_s, exp_t)):
                x = score[p * PIECE:(p + 1) * PIECE].reshape(PIECE // 8, 8, QUERIES)
                peak = jnp.max(x, axis=0)
                e = jnp.exp2((x - peak[None]) * rate)
                store[block % 2, here, :] = e.reshape(PIECE, QUERIES)
                stat.append((peak, jnp.sum(e, axis=0)))
            stats.append(stat)
        return stats

    def factors(stats):
        out = []
        for side in range(2):
            peaks = [stat[side][0] for stat in stats]
            top = peaks[0]
            for peak in peaks[1:]:
                top = jnp.maximum(top, peak)
            top = jnp.max(top, axis=0, keepdims=True)
            scale = [jnp.exp2((peak - top) * rates[side]) for peak in peaks]
            total = scale[0] * stats[0][side][1]
            for f, stat in zip(scale[1:], stats[1:]):
                total = total + f * stat[side][1]
            norm = 1.0 / jnp.sum(total, axis=0, keepdims=True)
            out.append([f * norm for f in scale])
        return out

    stats = [stat for half in range(halves) for stat in exps(0, half)]
    for block in range(blocks):
        slot = block % 2
        cols = pl.ds(block * QUERIES, QUERIES)
        scale_s, scale_t = factors(stats)
        stats = []
        for half in range(halves):
            if block + 1 < blocks:
                stats += exps(block + 1, half)
            for p in range(half * pieces, (half + 1) * pieces):
                here = pl.ds(p * PIECE, PIECE)
                s = exp_s[slot, here, :].reshape(PIECE // 8, 8, QUERIES) * scale_s[p][None]
                t = exp_t[slot, here, :].reshape(PIECE // 8, 8, QUERIES) * scale_t[p][None]
                mix[here, :] = (s - t).reshape(PIECE, QUERIES).astype(jnp.bfloat16)
            rows = pl.ds(half * HALF, HALF)
            g = dot(mix[rows, :], q_ref[cols, :], NN)
            if block == 0:
                acc[rows, :] = g
            else:
                acc[rows, :] += g
        gq = dot(turned[HDS:], mix[...], NN) * HDS ** -0.5
        grads[:HDS, cols] = gq.astype(jnp.bfloat16)
    grads[HDS:, :] = acc[...].T.astype(jnp.bfloat16)
    fetch.wait()
    for ref in prior:
        pltpu.make_async_copy(ref, prior_ref, sems.at[4]).wait()
    size = out_ref.shape[2]
    for d in range(out_ref.shape[0]):
        weight = dot(grads[...], x_ref[:, d * size:(d + 1) * size], NN)
        out_ref[d] = prior_ref[d] + weight if batch else weight


def relation_grads(head, batch, place, store, arrivals, pairs, inputs, prior, data_ways):
    tokens, width = inputs.shape[1:]
    relays = len(arrivals) // 2
    return pl.pallas_call(
        functools.partial(relation_kernel, head, batch, relays),
        grid=(1,),
        out_shape=jax.ShapeDtypeStruct((data_ways, 2 * HDS, width // data_ways), jnp.float32),
        in_specs=[pl.BlockSpec(memory_space=pltpu.SMEM)]
        + [pl.BlockSpec(memory_space=pl.ANY)] * (3 + len(arrivals) + len(prior)),
        out_specs=pl.BlockSpec((data_ways, 2 * HDS, width // data_ways), lambda u: (0, 0, 0)),
        scratch_shapes=[
            pltpu.VMEM((2, tokens, HDT), jnp.bfloat16),
            pltpu.VMEM((tokens, width), jnp.bfloat16),
            pltpu.VMEM((tokens, 2 * HDS), jnp.bfloat16),
            pltpu.VMEM((data_ways, 2 * HDS, width // data_ways), jnp.float32),
            pltpu.VMEM((tokens, HDS), jnp.bfloat16),
            pltpu.VMEM((tokens, HDS), jnp.bfloat16),
            pltpu.VMEM((2 * HDS, tokens), jnp.bfloat16),
            pltpu.VMEM((HDT, tokens), jnp.bfloat16),
            pltpu.VMEM((2, tokens, QUERIES), jnp.float32),
            pltpu.VMEM((2, tokens, QUERIES), jnp.float32),
            pltpu.VMEM((tokens, QUERIES), jnp.bfloat16),
            pltpu.VMEM((tokens, HDS), jnp.float32),
            pltpu.VMEM((2 * HDS, tokens), jnp.bfloat16),
            pltpu.SemaphoreType.DMA((5,)),
        ],
        compiler_params=pltpu.CompilerParams(vmem_limit_bytes=56 << 20),
        cost_estimate=pl.CostEstimate(flops=100_000_000, bytes_accessed=1 << 18, transcendentals=0),
    )(place, store, *arrivals, pairs, inputs, *prior)


def pair_kernel(head, relays, place_ref, store_ref, *refs):
    count = 2 * relays
    arrivals = refs[:count]
    pair_ref, x_hbm, out_ref = refs[count:count + 3]
    panel, x_ref, q_ref, k_ref, turned, turned_t, exp_s, exp_t, mix, acc, grads, sems = refs[count + 3:]
    tokens = k_ref.shape[1]

    def start(source, b, part):
        pltpu.make_async_copy(source, panel.at[b, part], sems.at[b]).start()

    for b in range(2):
        @pl.when(place_ref[0, b] == 0)
        def _():
            for part in range(2):
                start(store_ref.at[place_ref[1, b], 0, part, :, pl.ds(head * HDT, HDT)], b, part)

        for d in range(relays):
            @pl.when(place_ref[0, b] == d + 1)
            def _():
                for part in range(2):
                    start(arrivals[2 * d + part].at[b], b, part)
    fetch = pltpu.make_async_copy(x_hbm, x_ref, sems.at[2])
    fetch.start()
    blocks = tokens // QUERIES
    halves = tokens // HALF
    pieces = HALF // PIECE
    rates = (LOG2E, HDT ** -0.5 * LOG2E)

    def prepare(b):
        pair = pair_ref[b, 0]
        q_ref[b] = pair[:, :HDS] * jnp.bfloat16(HDS ** -0.5)
        k_ref[b] = pair[:, HDS:]
        turned[b] = pair.T
        turned[b, :HDS] = turned[b, :HDS] * jnp.bfloat16(HDS ** -0.5)
        pltpu.make_async_copy(panel.at[b], panel.at[b], sems.at[b]).wait()
        turned_t[b] = panel[b, 0].T

    def exps(step, half):
        b, block = divmod(step, blocks)
        cols = pl.ds(block * QUERIES, QUERIES)
        rows = pl.ds(half * HALF, HALF)
        both = (dot(k_ref[b, rows, :], turned[b, :HDS, cols], NN), dot(panel[b, 1, rows, :], turned_t[b, :, cols], NN))
        stats = []
        for p in range(pieces):
            here = pl.ds(half * HALF + p * PIECE, PIECE)
            stat = []
            for score, rate, store in zip(both, rates, (exp_s, exp_t)):
                x = score[p * PIECE:(p + 1) * PIECE].reshape(PIECE // 8, 8, QUERIES)
                peak = jnp.max(x, axis=0)
                e = jnp.exp2((x - peak[None]) * rate)
                store[step % 2, here, :] = e.reshape(PIECE, QUERIES)
                stat.append((peak, jnp.sum(e, axis=0)))
            stats.append(stat)
        return stats

    def factors(stats):
        out = []
        for side in range(2):
            peaks = [stat[side][0] for stat in stats]
            top = peaks[0]
            for peak in peaks[1:]:
                top = jnp.maximum(top, peak)
            top = jnp.max(top, axis=0, keepdims=True)
            scale = [jnp.exp2((peak - top) * rates[side]) for peak in peaks]
            total = scale[0] * stats[0][side][1]
            for f, stat in zip(scale[1:], stats[1:]):
                total = total + f * stat[side][1]
            norm = 1.0 / jnp.sum(total, axis=0, keepdims=True)
            out.append([f * norm for f in scale])
        return out

    prepare(0)
    stats = [stat for half in range(halves) for stat in exps(0, half)]
    for step in range(2 * blocks):
        b, block = divmod(step, blocks)
        slot = step % 2
        cols = pl.ds(block * QUERIES, QUERIES)
        scale_s, scale_t = factors(stats)
        stats = []
        if step + 1 == blocks:
            prepare(1)
        for half in range(halves):
            if step + 1 < 2 * blocks:
                stats += exps(step + 1, half)
            for p in range(half * pieces, (half + 1) * pieces):
                here = pl.ds(p * PIECE, PIECE)
                s = exp_s[slot, here, :].reshape(PIECE // 8, 8, QUERIES) * scale_s[p][None]
                t = exp_t[slot, here, :].reshape(PIECE // 8, 8, QUERIES) * scale_t[p][None]
                mix[slot, here, :] = (s - t).reshape(PIECE, QUERIES).astype(jnp.bfloat16)
            rows = pl.ds(half * HALF, HALF)
            g = dot(mix[slot, rows, :], q_ref[b, cols, :], NN)
            if block == 0:
                acc[rows, :] = g
            else:
                acc[rows, :] += g
        gq = dot(turned[b, HDS:], mix[slot], NN) * HDS ** -0.5
        grads[:HDS, pl.ds(step * QUERIES, QUERIES)] = gq.astype(jnp.bfloat16)
        if block + 1 == blocks:
            grads[HDS:, pl.ds(b * tokens, tokens)] = acc[...].T.astype(jnp.bfloat16)
    fetch.wait()
    size = out_ref.shape[2]
    for d in range(out_ref.shape[0]):
        cols = pl.ds(d * size, size)
        out_ref[d] = (dot(grads[:, :tokens], x_ref[0, :, cols], NN)
                      + dot(grads[:, tokens:], x_ref[1, :, cols], NN))


def paired_grads(head, place, store, arrivals, pairs, inputs, data_ways):
    tokens, width = inputs.shape[1:]
    return pl.pallas_call(
        functools.partial(pair_kernel, head, len(arrivals) // 2),
        grid=(1,),
        out_shape=jax.ShapeDtypeStruct((data_ways, 2 * HDS, width // data_ways), jnp.float32),
        in_specs=[pl.BlockSpec(memory_space=pltpu.SMEM)]
        + [pl.BlockSpec(memory_space=pl.ANY)] * (1 + len(arrivals))
        + [
            pl.BlockSpec((2, 1, tokens, 2 * HDS), lambda u: (0, head, 0, 0)),
            pl.BlockSpec(memory_space=pl.ANY),
        ],
        out_specs=pl.BlockSpec((data_ways, 2 * HDS, width // data_ways), lambda u: (0, 0, 0)),
        scratch_shapes=[
            pltpu.VMEM((2, 2, tokens, HDT), jnp.bfloat16),
            pltpu.VMEM((2, tokens, width), jnp.bfloat16),
            pltpu.VMEM((2, tokens, HDS), jnp.bfloat16),
            pltpu.VMEM((2, tokens, HDS), jnp.bfloat16),
            pltpu.VMEM((2, 2 * HDS, tokens), jnp.bfloat16),
            pltpu.VMEM((2, HDT, tokens), jnp.bfloat16),
            pltpu.VMEM((2, tokens, QUERIES), jnp.float32),
            pltpu.VMEM((2, tokens, QUERIES), jnp.float32),
            pltpu.VMEM((2, tokens, QUERIES), jnp.bfloat16),
            pltpu.VMEM((tokens, HDS), jnp.float32),
            pltpu.VMEM((2 * HDS, 2 * tokens), jnp.bfloat16),
            pltpu.SemaphoreType.DMA((3,)),
        ],
        compiler_params=pltpu.CompilerParams(vmem_limit_bytes=56 << 20),
        cost_estimate=pl.CostEstimate(flops=100_000_000, bytes_accessed=1 << 18, transcendentals=0),
    )(place, store, *arrivals, pairs, inputs)


def projection_kernel(order_ref, own_ref, far_ref, near_ref, last_ref, x_ref, out_ref, weights):
    @pl.when(pl.program_id(0) == 0)
    def _():
        size = own_ref.shape[0]
        for r, rows in enumerate((own_ref, far_ref, near_ref, last_ref)):
            weights[pl.ds(pl.multiple_of(order_ref[r] * size, size), size), :] = rows[...]

    for c in range(out_ref.shape[1] // 2):
        pair = dot(x_ref[0], weights[:, 4 * c * HDS:4 * (c + 1) * HDS], NN).astype(jnp.bfloat16)
        out_ref[0, 2 * c] = pair[:, :2 * HDS]
        out_ref[0, 2 * c + 1] = pair[:, 2 * HDS:]


def pick_kernel(targets_ref, table_ref, out_ref, sem):
    cols = table_ref.shape[2]
    copies = [pltpu.make_async_copy(table_ref.at[targets_ref[h]], out_ref.at[:, pl.ds(h * cols, cols)], sem.at[h])
              for h in range(out_ref.shape[1] // cols)]
    for copy in copies:
        copy.start()
    for copy in copies:
        copy.wait()


def pick(table, targets):
    rows, cols = table.shape[1:]
    count = targets.shape[0]
    return pl.pallas_call(
        pick_kernel,
        in_specs=[pl.BlockSpec(memory_space=pltpu.SMEM), pl.BlockSpec(memory_space=pl.ANY)],
        out_specs=pl.BlockSpec(memory_space=pltpu.VMEM),
        out_shape=jax.ShapeDtypeStruct((rows, count * cols), table.dtype),
        scratch_shapes=[pltpu.SemaphoreType.DMA((count,))],
        cost_estimate=pl.CostEstimate(flops=0, bytes_accessed=1 << 20, transcendentals=0),
    )(targets, table)


def slots_kernel(targets_ref, first_ref, last_ref, out_ref):
    parts = [ref.at[h] for ref in (first_ref, last_ref) for h in range(ref.shape[0])]
    for s in range(out_ref.shape[0]):
        total = jnp.where(targets_ref[0] == s, parts[0][...], 0.0)
        for h in range(1, len(parts)):
            total = total + jnp.where(targets_ref[h] == s, parts[h][...], 0.0)
        out_ref[s] = total.astype(out_ref.dtype)


def add_slots(targets, first, last, count):
    return pl.pallas_call(
        slots_kernel,
        in_specs=[pl.BlockSpec(memory_space=pltpu.SMEM)] + [pl.BlockSpec(memory_space=pltpu.VMEM)] * 2,
        out_specs=pl.BlockSpec(memory_space=pltpu.VMEM),
        out_shape=jax.ShapeDtypeStruct((count, *first.shape[1:]), jnp.bfloat16),
        cost_estimate=pl.CostEstimate(flops=0, bytes_accessed=1 << 20, transcendentals=0),
    )(targets, first, last)


def project(inputs, block, data):
    near = [(d, d ^ 1) for d in range(4)]
    far = [(d, d ^ 2) for d in range(4)]
    across = lax.ppermute(block, "dp", far)
    beside = lax.ppermute(block, "dp", near)
    last = lax.ppermute(across, "dp", near)
    order = jnp.stack([data, data ^ 2, data ^ 1, data ^ 3])
    batches, tokens, width = inputs.shape
    rows, cols = block.shape
    return pl.pallas_call(
        projection_kernel,
        grid=(batches,),
        out_shape=jax.ShapeDtypeStruct((batches, cols // (2 * HDS), tokens, 2 * HDS), jnp.bfloat16),
        in_specs=[
            pl.BlockSpec(memory_space=pltpu.SMEM),
            *[pl.BlockSpec((rows, cols), lambda b: (0, 0))] * 4,
            pl.BlockSpec((1, tokens, width), lambda b: (b, 0, 0)),
        ],
        out_specs=pl.BlockSpec((1, cols // (2 * HDS), tokens, 2 * HDS), lambda b: (b, 0, 0, 0)),
        scratch_shapes=[pltpu.VMEM((width, cols), jnp.bfloat16)],
        compiler_params=pltpu.CompilerParams(vmem_limit_bytes=56 << 20),
        cost_estimate=pl.CostEstimate(flops=4_000_000_000, bytes_accessed=8 << 20, transcendentals=0),
    )(order, block, across, beside, last, inputs)


def body(teacher_panels, owner_plan, head_map, student_input, student_weights):
    model_ways = lax.axis_size("mp")
    data_ways = lax.axis_size("dp")
    groups = lax.axis_size("group")
    column = lax.axis_index("mp")
    data = lax.axis_index("dp")
    store_slots = teacher_panels.shape[0]
    tokens = teacher_panels.shape[3]
    heads = teacher_panels.shape[4] // HDT
    width = student_input.shape[-1]
    row_block = width // data_ways
    column_block = width // model_ways
    column_heads = column_block // HDS
    targets = lax.dynamic_slice_in_dim(head_map[:, 0], column * heads, heads)

    here = lax.axis_index("group")
    owner = owner_plan // store_slots
    dist = jnp.where(data % 2 == 0, here - owner, owner - here) % groups
    slot = owner_plan % store_slots
    place = jnp.stack([dist, slot])
    ring = [(z * data_ways + d, (z + (1 if d % 2 == 0 else -1)) % groups * data_ways + d)
            for z in range(groups) for d in range(data_ways)]

    def held(store, part, start, count):
        pick = [lax.dynamic_slice(store, (slot[b], 0, part, 0, start), (1, 1, 1, tokens, count)) for b in range(2)]
        return jnp.concatenate(pick)[:, 0, 0]

    first = [held(teacher_panels, chunk, 0, HDT) for chunk in range(LAG)]
    first, student_weights, store = lax.optimization_barrier((first, student_weights, teacher_panels))

    table = student_weights[0].reshape(2, row_block, column_heads, HDS).transpose(2, 1, 0, 3)
    table = table.reshape(1, column_heads, row_block, 2 * HDS)
    table = lax.all_to_all(jnp.broadcast_to(table, (model_ways, *table.shape[1:])), "mp", 0, 0, tiled=True)

    own = [held(store, part, HDT, (heads - 1) * HDT) for part in range(2)]
    chunks = 2 * heads
    stages = chunks + LAG * (groups - 2)
    lead = 1 + LAG * (groups - 2)
    inputs = student_input[0, :, 0]
    arrived = []
    pairs = None
    pieces = []

    def sources(head):
        return [arrived[2 * head + part + LAG * d] for d in range(groups - 1) for part in range(2)]

    def grad(unit, place):
        head, b = divmod(unit, 2)
        return relation_grads(head, b, place, teacher_panels, sources(head), pairs, inputs, pieces[-1:] * b, data_ways)

    for stage in range(stages):
        if stage < LAG:
            send = first[stage]
        else:
            passed = arrived[stage - LAG]
            if stage == LAG + 1:
                passed, table, own = lax.optimization_barrier((passed, table, own))
                mine = pick(table.reshape(model_ways * column_heads, row_block, 2 * HDS), targets)
                pairs = project(inputs, mine, data)
            head, part = divmod(min(stage, chunks - 1), 2)
            mine = own[part][:, :, (head - 1) * HDT:head * HDT]
            send = jnp.where((dist == 0)[:, None, None], mine, passed)
            send, own = lax.optimization_barrier((send, own))
        unit = stage - lead - LAG - 1
        if unit >= 0:
            piece, send, place = lax.optimization_barrier((grad(unit, place), send, place))
            pieces.append(piece)
        arrived.append(lax.ppermute(send, ("group", "dp"), ring))
    early = len(pieces) // 2
    reduced = reduce_data(pieces[1::2], data, jnp.float32)
    final = []
    for head in range(early, heads):
        if head == heads - 1:
            reduced, place = lax.optimization_barrier((reduced, place))
        piece = paired_grads(head, place, teacher_panels, sources(head), pairs, inputs, data_ways)
        piece, place = lax.optimization_barrier((piece, place))
        final.append(piece)

    final = reduce_data(final, data, jnp.bfloat16)
    slots = add_slots(targets, reduced, final, model_ways * column_heads)
    slots = slots.reshape(model_ways, column_heads, 2 * HDS, row_block)
    slots = lax.all_to_all(slots, "mp", 0, 0, tiled=True)
    result = jnp.sum(slots.astype(jnp.float32), axis=0).reshape(column_heads, 2, HDS, row_block)
    return result.transpose(1, 3, 0, 2).reshape(1, 2, row_block, column_block)


def reduce_data(pieces, data, dtype):
    near = [(d, d ^ 1) for d in range(4)]
    far = [(d, d ^ 2) for d in range(4)]
    core = data % 2
    chip = data // 2
    halves = [piece.reshape(2, 2, *piece.shape[1:]) for piece in pieces]

    def half(which):
        return jnp.stack([lax.dynamic_index_in_dim(piece, which, 1, keepdims=False) for piece in halves], axis=1)

    kept = half(core) + lax.ppermute(half(1 - core), "dp", near)
    got = lax.ppermute(lax.dynamic_index_in_dim(kept, 1 - chip, 0, keepdims=False).astype(dtype), "dp", far)
    return lax.dynamic_index_in_dim(kept, chip, 0, keepdims=False) + got.astype(jnp.float32)


def solution(mesh):
    in_specs = (
        P("group", "dp", None, None, "mp"),
        P(),
        P(),
        P("group", None, "dp", None, None),
        P("group", None, "dp", "mp"),
    )
    out_specs = P("group", None, "dp", "mp")
    return jax.shard_map(body, mesh=mesh, in_specs=in_specs, out_specs=out_specs, check_vma=False)
```

```python
import functools

import jax
import jax.numpy as jnp
from jax import lax
from jax.experimental import pallas as pl
from jax.experimental.pallas import tpu as pltpu
from jax.sharding import PartitionSpec as P

HDT = 128
HDS = 64
LOG2E = 1.4426950408889634
QUERIES = 256
HALF = 512
PIECE = 64
PARTS = 4
LAG = 2
NN = (((1,), (0,)), ((), ()))


def dot(a, b, dims):
    return lax.dot_general(a, b, dims, preferred_element_type=jnp.float32)


def copy_parts(source, target, sem):
    size = target.shape[0] // PARTS
    for part in range(PARTS):
        rows = pl.ds(part * size, size)
        pltpu.make_async_copy(source.at[rows], target.at[rows], sem).start()


def wait_parts(target, sem):
    pltpu.make_async_copy(target, target, sem).wait()


def relation_kernel(head, batch, relays, place_ref, store_ref, *refs):
    arrivals = refs[:2 * relays]
    pair_hbm, x_hbm = refs[2 * relays:2 * relays + 2]
    refs = refs[2 * relays + 2:]
    prior = refs[:batch]
    out_hbm = refs[batch]
    panel, x_ref, pair_ref, prior_ref, out_ref, q_ref, k_ref, turned, turned_t, exp_s, exp_t, mix, acc, grads, sems = refs[batch + 1:]
    tokens = k_ref.shape[0]

    @pl.when(place_ref[0, batch] == 0)
    def _():
        for part in range(2):
            held = store_ref.at[place_ref[1, batch], 0, part, :, pl.ds(head * HDT, HDT)]
            copy_parts(held, panel.at[part], sems.at[part])

    for d in range(relays):
        @pl.when(place_ref[0, batch] == d + 1)
        def _():
            for part in range(2):
                copy_parts(arrivals[2 * d + part].at[batch], panel.at[part], sems.at[part])

    copy_parts(pair_hbm.at[batch, head], pair_ref, sems.at[3])
    wait_parts(pair_ref, sems.at[3])
    pair = pair_ref[...]
    q_ref[...] = pair[:, :HDS] * jnp.bfloat16(HDS ** -0.5)
    k_ref[...] = pair[:, HDS:]
    turned[...] = pair.T
    turned[:HDS] = turned[:HDS] * jnp.bfloat16(HDS ** -0.5)
    for part in range(2):
        wait_parts(panel.at[part], sems.at[part])
    copy_parts(x_hbm.at[batch], x_ref, sems.at[2])
    for ref in prior:
        copy_parts(ref, prior_ref, sems.at[4])
    turned_t[...] = panel[0].T
    blocks = tokens // QUERIES
    halves = tokens // HALF
    pieces = HALF // PIECE
    rates = (LOG2E, HDT ** -0.5 * LOG2E)

    def exps(block, half):
        cols = pl.ds(block * QUERIES, QUERIES)
        rows = pl.ds(half * HALF, HALF)
        both = (dot(k_ref[rows, :], turned[:HDS, cols], NN), dot(panel[1, rows, :], turned_t[:, cols], NN))
        stats = []
        for p in range(pieces):
            here = pl.ds(half * HALF + p * PIECE, PIECE)
            stat = []
            for score, rate, store in zip(both, rates, (exp_s, exp_t)):
                x = score[p * PIECE:(p + 1) * PIECE].reshape(PIECE // 8, 8, QUERIES)
                peak = jnp.max(x, axis=0)
                e = jnp.exp2((x - peak[None]) * rate)
                store[block % 2, here, :] = e.reshape(PIECE, QUERIES)
                stat.append((peak, jnp.sum(e, axis=0)))
            stats.append(stat)
        return stats

    def factors(stats):
        out = []
        for side in range(2):
            peaks = [stat[side][0] for stat in stats]
            top = peaks[0]
            for peak in peaks[1:]:
                top = jnp.maximum(top, peak)
            top = jnp.max(top, axis=0, keepdims=True)
            scale = [jnp.exp2((peak - top) * rates[side]) for peak in peaks]
            total = scale[0] * stats[0][side][1]
            for f, stat in zip(scale[1:], stats[1:]):
                total = total + f * stat[side][1]
            norm = 1.0 / jnp.sum(total, axis=0, keepdims=True)
            out.append([f * norm for f in scale])
        return out

    stats = [stat for half in range(halves) for stat in exps(0, half)]
    for block in range(blocks):
        slot = block % 2
        cols = pl.ds(block * QUERIES, QUERIES)
        scale_s, scale_t = factors(stats)
        stats = []
        for half in range(halves):
            if block + 1 < blocks:
                stats += exps(block + 1, half)
            for p in range(half * pieces, (half + 1) * pieces):
                here = pl.ds(p * PIECE, PIECE)
                s = exp_s[slot, here, :].reshape(PIECE // 8, 8, QUERIES) * scale_s[p][None]
                t = exp_t[slot, here, :].reshape(PIECE // 8, 8, QUERIES) * scale_t[p][None]
                mix[here, :] = (s - t).reshape(PIECE, QUERIES).astype(jnp.bfloat16)
            rows = pl.ds(half * HALF, HALF)
            g = dot(mix[rows, :], q_ref[cols, :], NN)
            if block == 0:
                acc[rows, :] = g
            else:
                acc[rows, :] += g
        gq = dot(turned[HDS:], mix[...], NN) * HDS ** -0.5
        grads[:HDS, cols] = gq.astype(jnp.bfloat16)
    grads[HDS:, :] = acc[...].T.astype(jnp.bfloat16)
    wait_parts(x_ref, sems.at[2])
    for ref in prior:
        wait_parts(prior_ref, sems.at[4])
    size = out_ref.shape[2]
    for d in range(out_ref.shape[0]):
        weight = dot(grads[...], x_ref[:, d * size:(d + 1) * size], NN)
        out_ref[d] = prior_ref[d] + weight if batch else weight
        pltpu.make_async_copy(out_ref.at[d], out_hbm.at[d], sems.at[5]).start()
    pltpu.make_async_copy(out_ref, out_hbm, sems.at[5]).wait()


def relation_grads(head, batch, place, store, arrivals, pairs, inputs, prior, data_ways):
    tokens, width = inputs.shape[1:]
    relays = len(arrivals) // 2
    return pl.pallas_call(
        functools.partial(relation_kernel, head, batch, relays),
        grid=(1,),
        out_shape=jax.ShapeDtypeStruct((data_ways, 2 * HDS, width // data_ways), jnp.float32),
        in_specs=[pl.BlockSpec(memory_space=pltpu.SMEM)]
        + [pl.BlockSpec(memory_space=pl.ANY)] * (3 + len(arrivals) + len(prior)),
        out_specs=pl.BlockSpec(memory_space=pl.ANY),
        scratch_shapes=[
            pltpu.VMEM((2, tokens, HDT), jnp.bfloat16),
            pltpu.VMEM((tokens, width), jnp.bfloat16),
            pltpu.VMEM((tokens, 2 * HDS), jnp.bfloat16),
            *[pltpu.VMEM((data_ways, 2 * HDS, width // data_ways), jnp.float32)] * 2,
            pltpu.VMEM((tokens, HDS), jnp.bfloat16),
            pltpu.VMEM((tokens, HDS), jnp.bfloat16),
            pltpu.VMEM((2 * HDS, tokens), jnp.bfloat16),
            pltpu.VMEM((HDT, tokens), jnp.bfloat16),
            pltpu.VMEM((2, tokens, QUERIES), jnp.float32),
            pltpu.VMEM((2, tokens, QUERIES), jnp.float32),
            pltpu.VMEM((tokens, QUERIES), jnp.bfloat16),
            pltpu.VMEM((tokens, HDS), jnp.float32),
            pltpu.VMEM((2 * HDS, tokens), jnp.bfloat16),
            pltpu.SemaphoreType.DMA((6,)),
        ],
        compiler_params=pltpu.CompilerParams(vmem_limit_bytes=56 << 20),
        cost_estimate=pl.CostEstimate(flops=100_000_000, bytes_accessed=1 << 18, transcendentals=0),
    )(place, store, *arrivals, pairs, inputs, *prior)


def pair_kernel(head, relays, place_ref, store_ref, *refs):
    count = 2 * relays
    arrivals = refs[:count]
    pair_ref, x_hbm, out_ref = refs[count:count + 3]
    panel, x_ref, q_ref, k_ref, turned, turned_t, exp_s, exp_t, mix, acc, grads, sems = refs[count + 3:]
    tokens = k_ref.shape[1]

    def start(source, b, part):
        copy_parts(source, panel.at[b, part], sems.at[b])

    for b in range(2):
        @pl.when(place_ref[0, b] == 0)
        def _():
            for part in range(2):
                start(store_ref.at[place_ref[1, b], 0, part, :, pl.ds(head * HDT, HDT)], b, part)

        for d in range(relays):
            @pl.when(place_ref[0, b] == d + 1)
            def _():
                for part in range(2):
                    start(arrivals[2 * d + part].at[b], b, part)
    fetch = pltpu.make_async_copy(x_hbm, x_ref, sems.at[2])
    fetch.start()
    blocks = tokens // QUERIES
    halves = tokens // HALF
    pieces = HALF // PIECE
    rates = (LOG2E, HDT ** -0.5 * LOG2E)

    def prepare(b):
        pair = pair_ref[b, 0]
        q_ref[b] = pair[:, :HDS] * jnp.bfloat16(HDS ** -0.5)
        k_ref[b] = pair[:, HDS:]
        turned[b] = pair.T
        turned[b, :HDS] = turned[b, :HDS] * jnp.bfloat16(HDS ** -0.5)
        pltpu.make_async_copy(panel.at[b], panel.at[b], sems.at[b]).wait()
        turned_t[b] = panel[b, 0].T

    def exps(step, half):
        b, block = divmod(step, blocks)
        cols = pl.ds(block * QUERIES, QUERIES)
        rows = pl.ds(half * HALF, HALF)
        both = (dot(k_ref[b, rows, :], turned[b, :HDS, cols], NN), dot(panel[b, 1, rows, :], turned_t[b, :, cols], NN))
        stats = []
        for p in range(pieces):
            here = pl.ds(half * HALF + p * PIECE, PIECE)
            stat = []
            for score, rate, store in zip(both, rates, (exp_s, exp_t)):
                x = score[p * PIECE:(p + 1) * PIECE].reshape(PIECE // 8, 8, QUERIES)
                peak = jnp.max(x, axis=0)
                e = jnp.exp2((x - peak[None]) * rate)
                store[step % 2, here, :] = e.reshape(PIECE, QUERIES)
                stat.append((peak, jnp.sum(e, axis=0)))
            stats.append(stat)
        return stats

    def factors(stats):
        out = []
        for side in range(2):
            peaks = [stat[side][0] for stat in stats]
            top = peaks[0]
            for peak in peaks[1:]:
                top = jnp.maximum(top, peak)
            top = jnp.max(top, axis=0, keepdims=True)
            scale = [jnp.exp2((peak - top) * rates[side]) for peak in peaks]
            total = scale[0] * stats[0][side][1]
            for f, stat in zip(scale[1:], stats[1:]):
                total = total + f * stat[side][1]
            norm = 1.0 / jnp.sum(total, axis=0, keepdims=True)
            out.append([f * norm for f in scale])
        return out

    prepare(0)
    stats = [stat for half in range(halves) for stat in exps(0, half)]
    for step in range(2 * blocks):
        b, block = divmod(step, blocks)
        slot = step % 2
        cols = pl.ds(block * QUERIES, QUERIES)
        scale_s, scale_t = factors(stats)
        stats = []
        if step + 1 == blocks:
            prepare(1)
        for half in range(halves):
            if step + 1 < 2 * blocks:
                stats += exps(step + 1, half)
            for p in range(half * pieces, (half + 1) * pieces):
                here = pl.ds(p * PIECE, PIECE)
                s = exp_s[slot, here, :].reshape(PIECE // 8, 8, QUERIES) * scale_s[p][None]
                t = exp_t[slot, here, :].reshape(PIECE // 8, 8, QUERIES) * scale_t[p][None]
                mix[slot, here, :] = (s - t).reshape(PIECE, QUERIES).astype(jnp.bfloat16)
            rows = pl.ds(half * HALF, HALF)
            g = dot(mix[slot, rows, :], q_ref[b, cols, :], NN)
            if block == 0:
                acc[rows, :] = g
            else:
                acc[rows, :] += g
        gq = dot(turned[b, HDS:], mix[slot], NN) * HDS ** -0.5
        grads[:HDS, pl.ds(step * QUERIES, QUERIES)] = gq.astype(jnp.bfloat16)
        if block + 1 == blocks:
            grads[HDS:, pl.ds(b * tokens, tokens)] = acc[...].T.astype(jnp.bfloat16)
    fetch.wait()
    size = out_ref.shape[2]
    for d in range(out_ref.shape[0]):
        cols = pl.ds(d * size, size)
        out_ref[d] = (dot(grads[:, :tokens], x_ref[0, :, cols], NN)
                      + dot(grads[:, tokens:], x_ref[1, :, cols], NN))


def paired_grads(head, place, store, arrivals, pairs, inputs, data_ways):
    tokens, width = inputs.shape[1:]
    return pl.pallas_call(
        functools.partial(pair_kernel, head, len(arrivals) // 2),
        grid=(1,),
        out_shape=jax.ShapeDtypeStruct((data_ways, 2 * HDS, width // data_ways), jnp.float32),
        in_specs=[pl.BlockSpec(memory_space=pltpu.SMEM)]
        + [pl.BlockSpec(memory_space=pl.ANY)] * (1 + len(arrivals))
        + [
            pl.BlockSpec((2, 1, tokens, 2 * HDS), lambda u: (0, head, 0, 0)),
            pl.BlockSpec(memory_space=pl.ANY),
        ],
        out_specs=pl.BlockSpec((data_ways, 2 * HDS, width // data_ways), lambda u: (0, 0, 0)),
        scratch_shapes=[
            pltpu.VMEM((2, 2, tokens, HDT), jnp.bfloat16),
            pltpu.VMEM((2, tokens, width), jnp.bfloat16),
            pltpu.VMEM((2, tokens, HDS), jnp.bfloat16),
            pltpu.VMEM((2, tokens, HDS), jnp.bfloat16),
            pltpu.VMEM((2, 2 * HDS, tokens), jnp.bfloat16),
            pltpu.VMEM((2, HDT, tokens), jnp.bfloat16),
            pltpu.VMEM((2, tokens, QUERIES), jnp.float32),
            pltpu.VMEM((2, tokens, QUERIES), jnp.float32),
            pltpu.VMEM((2, tokens, QUERIES), jnp.bfloat16),
            pltpu.VMEM((tokens, HDS), jnp.float32),
            pltpu.VMEM((2 * HDS, 2 * tokens), jnp.bfloat16),
            pltpu.SemaphoreType.DMA((3,)),
        ],
        compiler_params=pltpu.CompilerParams(vmem_limit_bytes=56 << 20),
        cost_estimate=pl.CostEstimate(flops=100_000_000, bytes_accessed=1 << 18, transcendentals=0),
    )(place, store, *arrivals, pairs, inputs)


def projection_kernel(order_ref, own_ref, far_ref, near_ref, last_ref, x_ref, out_ref, weights):
    @pl.when((pl.program_id(0) == 0) & (pl.program_id(1) == 0))
    def _():
        size = own_ref.shape[0]
        for r, rows in enumerate((own_ref, far_ref, near_ref, last_ref)):
            weights[pl.ds(pl.multiple_of(order_ref[r] * size, size), size), :] = rows[...]

    for c in range(out_ref.shape[1] // 2):
        pair = dot(x_ref[0], weights[:, 4 * c * HDS:4 * (c + 1) * HDS], NN).astype(jnp.bfloat16)
        out_ref[0, 2 * c] = pair[:, :2 * HDS]
        out_ref[0, 2 * c + 1] = pair[:, 2 * HDS:]


def pick_kernel(targets_ref, table_ref, out_ref, sem):
    cols = table_ref.shape[2]
    copies = [pltpu.make_async_copy(table_ref.at[targets_ref[h]], out_ref.at[:, pl.ds(h * cols, cols)], sem.at[h])
              for h in range(out_ref.shape[1] // cols)]
    for copy in copies:
        copy.start()
    for copy in copies:
        copy.wait()


def pick(table, targets):
    rows, cols = table.shape[1:]
    count = targets.shape[0]
    return pl.pallas_call(
        pick_kernel,
        in_specs=[pl.BlockSpec(memory_space=pltpu.SMEM), pl.BlockSpec(memory_space=pl.ANY)],
        out_specs=pl.BlockSpec(memory_space=pltpu.VMEM),
        out_shape=jax.ShapeDtypeStruct((rows, count * cols), table.dtype),
        scratch_shapes=[pltpu.SemaphoreType.DMA((count,))],
        cost_estimate=pl.CostEstimate(flops=0, bytes_accessed=1 << 20, transcendentals=0),
    )(targets, table)


def slots_kernel(targets_ref, first_ref, last_ref, out_ref):
    parts = [ref.at[h] for ref in (first_ref, last_ref) for h in range(ref.shape[0])]
    for s in range(out_ref.shape[0]):
        total = jnp.where(targets_ref[0] == s, parts[0][...], 0.0)
        for h in range(1, len(parts)):
            total = total + jnp.where(targets_ref[h] == s, parts[h][...], 0.0)
        out_ref[s] = total.astype(out_ref.dtype)


def add_slots(targets, first, last, count):
    return pl.pallas_call(
        slots_kernel,
        in_specs=[pl.BlockSpec(memory_space=pltpu.SMEM)] + [pl.BlockSpec(memory_space=pltpu.VMEM)] * 2,
        out_specs=pl.BlockSpec(memory_space=pltpu.VMEM),
        out_shape=jax.ShapeDtypeStruct((count, *first.shape[1:]), jnp.bfloat16),
        cost_estimate=pl.CostEstimate(flops=0, bytes_accessed=1 << 20, transcendentals=0),
    )(targets, first, last)


def project(inputs, block, data):
    near = [(d, d ^ 1) for d in range(4)]
    far = [(d, d ^ 2) for d in range(4)]
    across = lax.ppermute(block, "dp", far)
    beside = lax.ppermute(block, "dp", near)
    last = lax.ppermute(across, "dp", near)
    order = jnp.stack([data, data ^ 2, data ^ 1, data ^ 3])
    batches, tokens, width = inputs.shape
    rows, cols = block.shape
    return pl.pallas_call(
        projection_kernel,
        grid=(batches, PARTS),
        out_shape=jax.ShapeDtypeStruct((batches, cols // (2 * HDS), tokens, 2 * HDS), jnp.bfloat16),
        in_specs=[
            pl.BlockSpec(memory_space=pltpu.SMEM),
            *[pl.BlockSpec((rows, cols), lambda b, r: (0, 0))] * 4,
            pl.BlockSpec((1, tokens // PARTS, width), lambda b, r: (b, r, 0)),
        ],
        out_specs=pl.BlockSpec((1, cols // (2 * HDS), tokens // PARTS, 2 * HDS), lambda b, r: (b, 0, r, 0)),
        scratch_shapes=[pltpu.VMEM((width, cols), jnp.bfloat16)],
        compiler_params=pltpu.CompilerParams(vmem_limit_bytes=56 << 20),
        cost_estimate=pl.CostEstimate(flops=4_000_000_000, bytes_accessed=8 << 20, transcendentals=0),
    )(order, block, across, beside, last, inputs)


def body(teacher_panels, owner_plan, head_map, student_input, student_weights):
    model_ways = lax.axis_size("mp")
    data_ways = lax.axis_size("dp")
    groups = lax.axis_size("group")
    column = lax.axis_index("mp")
    data = lax.axis_index("dp")
    store_slots = teacher_panels.shape[0]
    tokens = teacher_panels.shape[3]
    heads = teacher_panels.shape[4] // HDT
    width = student_input.shape[-1]
    row_block = width // data_ways
    column_block = width // model_ways
    column_heads = column_block // HDS
    targets = lax.dynamic_slice_in_dim(head_map[:, 0], column * heads, heads)

    here = lax.axis_index("group")
    owner = owner_plan // store_slots
    dist = jnp.where(data % 2 == 0, here - owner, owner - here) % groups
    slot = owner_plan % store_slots
    place = jnp.stack([dist, slot])
    ring = [(z * data_ways + d, (z + (1 if d % 2 == 0 else -1)) % groups * data_ways + d)
            for z in range(groups) for d in range(data_ways)]

    def held(store, part, start, count):
        pick = [lax.dynamic_slice(store, (slot[b], 0, part, 0, start), (1, 1, 1, tokens, count)) for b in range(2)]
        return jnp.concatenate(pick)[:, 0, 0]

    first = [held(teacher_panels, chunk, 0, HDT) for chunk in range(LAG)]
    first, student_weights, store = lax.optimization_barrier((first, student_weights, teacher_panels))

    table = student_weights[0].reshape(2, row_block, column_heads, HDS).transpose(2, 1, 0, 3)
    table = table.reshape(1, column_heads, row_block, 2 * HDS)
    table = lax.all_to_all(jnp.broadcast_to(table, (model_ways, *table.shape[1:])), "mp", 0, 0, tiled=True)

    own = [held(store, part, HDT, (heads - 1) * HDT) for part in range(2)]
    chunks = 2 * heads
    stages = chunks + LAG * (groups - 2)
    lead = 1 + LAG * (groups - 2)
    inputs = student_input[0, :, 0]
    arrived = []
    pairs = None
    pieces = []

    def sources(head):
        return [arrived[2 * head + part + LAG * d] for d in range(groups - 1) for part in range(2)]

    def grad(unit, place):
        head, b = divmod(unit, 2)
        return relation_grads(head, b, place, teacher_panels, sources(head), pairs, inputs, pieces[-1:] * b, data_ways)

    for stage in range(stages):
        if stage < LAG:
            send = first[stage]
        else:
            passed = arrived[stage - LAG]
            if stage == LAG + 1:
                passed, table, own = lax.optimization_barrier((passed, table, own))
                mine = pick(table.reshape(model_ways * column_heads, row_block, 2 * HDS), targets)
                pairs = project(inputs, mine, data)
            head, part = divmod(min(stage, chunks - 1), 2)
            mine = own[part][:, :, (head - 1) * HDT:head * HDT]
            send = jnp.where((dist == 0)[:, None, None], mine, passed)
            send, own = lax.optimization_barrier((send, own))
        unit = stage - lead - LAG - 1
        if unit >= 0:
            piece, send, place = lax.optimization_barrier((grad(unit, place), send, place))
            pieces.append(piece)
        arrived.append(lax.ppermute(send, ("group", "dp"), ring))
    early = len(pieces) // 2
    reduced = reduce_data(pieces[1::2], data, jnp.float32)
    final = []
    for head in range(early, heads):
        if head == heads - 1:
            reduced, place = lax.optimization_barrier((reduced, place))
        piece = paired_grads(head, place, teacher_panels, sources(head), pairs, inputs, data_ways)
        piece, place = lax.optimization_barrier((piece, place))
        final.append(piece)

    final = reduce_data(final, data, jnp.bfloat16)
    slots = add_slots(targets, reduced, final, model_ways * column_heads)
    slots = slots.reshape(model_ways, column_heads, 2 * HDS, row_block)
    slots = lax.all_to_all(slots, "mp", 0, 0, tiled=True)
    result = jnp.sum(slots.astype(jnp.float32), axis=0).reshape(column_heads, 2, HDS, row_block)
    return result.transpose(1, 3, 0, 2).reshape(1, 2, row_block, column_block)


def reduce_data(pieces, data, dtype):
    near = [(d, d ^ 1) for d in range(4)]
    far = [(d, d ^ 2) for d in range(4)]
    core = data % 2
    chip = data // 2
    halves = [piece.reshape(2, 2, *piece.shape[1:]) for piece in pieces]

    def half(which):
        return jnp.stack([lax.dynamic_index_in_dim(piece, which, 1, keepdims=False) for piece in halves], axis=1)

    kept = half(core) + lax.ppermute(half(1 - core), "dp", near)
    got = lax.ppermute(lax.dynamic_index_in_dim(kept, 1 - chip, 0, keepdims=False).astype(dtype), "dp", far)
    return lax.dynamic_index_in_dim(kept, chip, 0, keepdims=False) + got.astype(jnp.float32)


def solution(mesh):
    in_specs = (
        P("group", "dp", None, None, "mp"),
        P(),
        P(),
        P("group", None, "dp", None, None),
        P("group", None, "dp", "mp"),
    )
    out_specs = P("group", None, "dp", "mp")
    return jax.shard_map(body, mesh=mesh, in_specs=in_specs, out_specs=out_specs, check_vma=False)
```

```python
import functools

import jax
import jax.numpy as jnp
from jax import lax
from jax.experimental import pallas as pl
from jax.experimental.pallas import tpu as pltpu
from jax.sharding import PartitionSpec as P

HDT = 128
HDS = 64
LOG2E = 1.4426950408889634
QUERIES = 256
HALF = 512
PIECE = 64
LAG = 2
NN = (((1,), (0,)), ((), ()))


def dot(a, b, dims):
    return lax.dot_general(a, b, dims, preferred_element_type=jnp.float32)


def relation_kernel(head, batch, relays, place_ref, store_ref, *refs):
    arrivals = refs[:2 * relays]
    pair_hbm, x_hbm = refs[2 * relays:2 * relays + 2]
    refs = refs[2 * relays + 2:]
    prior = refs[:batch]
    out_ref = refs[batch]
    panel, x_ref, pair_ref, prior_ref, q_ref, k_ref, turned, turned_t, exp_s, exp_t, mix, acc, grads, sems = refs[batch + 1:]
    tokens = k_ref.shape[0]

    @pl.when(place_ref[0, batch] == 0)
    def _():
        for part in range(2):
            held = store_ref.at[place_ref[1, batch], 0, part, :, pl.ds(head * HDT, HDT)]
            pltpu.make_async_copy(held, panel.at[part], sems.at[part]).start()

    for d in range(relays):
        @pl.when(place_ref[0, batch] == d + 1)
        def _():
            for part in range(2):
                pltpu.make_async_copy(arrivals[2 * d + part].at[batch], panel.at[part], sems.at[part]).start()

    load = pltpu.make_async_copy(pair_hbm.at[batch, head], pair_ref, sems.at[3])
    load.start()
    load.wait()
    pair = pair_ref[...]
    q_ref[...] = pair[:, :HDS] * jnp.bfloat16(HDS ** -0.5)
    k_ref[...] = pair[:, HDS:]
    turned[...] = pair.T
    turned[:HDS] = turned[:HDS] * jnp.bfloat16(HDS ** -0.5)
    for part in range(2):
        pltpu.make_async_copy(arrivals[part].at[batch], panel.at[part], sems.at[part]).wait()
    fetch = pltpu.make_async_copy(x_hbm.at[batch], x_ref, sems.at[2])
    fetch.start()
    for ref in prior:
        pltpu.make_async_copy(ref, prior_ref, sems.at[4]).start()
    turned_t[...] = panel[0].T
    blocks = tokens // QUERIES
    halves = tokens // HALF
    pieces = HALF // PIECE
    rates = (LOG2E, HDT ** -0.5 * LOG2E)

    def exps(block, half):
        cols = pl.ds(block * QUERIES, QUERIES)
        rows = pl.ds(half * HALF, HALF)
        both = (dot(k_ref[rows, :], turned[:HDS, cols], NN), dot(panel[1, rows, :], turned_t[:, cols], NN))
        stats = []
        for p in range(pieces):
            here = pl.ds(half * HALF + p * PIECE, PIECE)
            stat = []
            for score, rate, store in zip(both, rates, (exp_s, exp_t)):
                x = score[p * PIECE:(p + 1) * PIECE].reshape(PIECE // 8, 8, QUERIES)
                peak = jnp.max(x, axis=0)
                e = jnp.exp2((x - peak[None]) * rate)
                store[block % 2, here, :] = e.reshape(PIECE, QUERIES)
                stat.append((peak, jnp.sum(e, axis=0)))
            stats.append(stat)
        return stats

    def factors(stats):
        out = []
        for side in range(2):
            peaks = [stat[side][0] for stat in stats]
            top = peaks[0]
            for peak in peaks[1:]:
                top = jnp.maximum(top, peak)
            top = jnp.max(top, axis=0, keepdims=True)
            scale = [jnp.exp2((peak - top) * rates[side]) for peak in peaks]
            total = scale[0] * stats[0][side][1]
            for f, stat in zip(scale[1:], stats[1:]):
                total = total + f * stat[side][1]
            norm = 1.0 / jnp.sum(total, axis=0, keepdims=True)
            out.append([f * norm for f in scale])
        return out

    stats = [stat for half in range(halves) for stat in exps(0, half)]
    for block in range(blocks):
        slot = block % 2
        cols = pl.ds(block * QUERIES, QUERIES)
        scale_s, scale_t = factors(stats)
        stats = []
        for half in range(halves):
            if block + 1 < blocks:
                stats += exps(block + 1, half)
            for p in range(half * pieces, (half + 1) * pieces):
                here = pl.ds(p * PIECE, PIECE)
                s = exp_s[slot, here, :].reshape(PIECE // 8, 8, QUERIES) * scale_s[p][None]
                t = exp_t[slot, here, :].reshape(PIECE // 8, 8, QUERIES) * scale_t[p][None]
                mix[here, :] = (s - t).reshape(PIECE, QUERIES).astype(jnp.bfloat16)
            rows = pl.ds(half * HALF, HALF)
            g = dot(mix[rows, :], q_ref[cols, :], NN)
            if block == 0:
                acc[rows, :] = g
            else:
                acc[rows, :] += g
        gq = dot(turned[HDS:], mix[...], NN) * HDS ** -0.5
        grads[:HDS, cols] = gq.astype(jnp.bfloat16)
    grads[HDS:, :] = acc[...].T.astype(jnp.bfloat16)
    fetch.wait()
    for ref in prior:
        pltpu.make_async_copy(ref, prior_ref, sems.at[4]).wait()
    size = out_ref.shape[2]
    for d in range(out_ref.shape[0]):
        weight = dot(grads[...], x_ref[:, d * size:(d + 1) * size], NN)
        out_ref[d] = prior_ref[d] + weight if batch else weight


def relation_grads(head, batch, place, store, arrivals, pairs, inputs, prior, data_ways):
    tokens, width = inputs.shape[1:]
    relays = len(arrivals) // 2
    return pl.pallas_call(
        functools.partial(relation_kernel, head, batch, relays),
        grid=(1,),
        out_shape=jax.ShapeDtypeStruct((data_ways, 2 * HDS, width // data_ways), jnp.float32),
        in_specs=[pl.BlockSpec(memory_space=pltpu.SMEM)]
        + [pl.BlockSpec(memory_space=pl.ANY)] * (3 + len(arrivals) + len(prior)),
        out_specs=pl.BlockSpec((data_ways, 2 * HDS, width // data_ways), lambda u: (0, 0, 0)),
        scratch_shapes=[
            pltpu.VMEM((2, tokens, HDT), jnp.bfloat16),
            pltpu.VMEM((tokens, width), jnp.bfloat16),
            pltpu.VMEM((tokens, 2 * HDS), jnp.bfloat16),
            pltpu.VMEM((data_ways, 2 * HDS, width // data_ways), jnp.float32),
            pltpu.VMEM((tokens, HDS), jnp.bfloat16),
            pltpu.VMEM((tokens, HDS), jnp.bfloat16),
            pltpu.VMEM((2 * HDS, tokens), jnp.bfloat16),
            pltpu.VMEM((HDT, tokens), jnp.bfloat16),
            pltpu.VMEM((2, tokens, QUERIES), jnp.float32),
            pltpu.VMEM((2, tokens, QUERIES), jnp.float32),
            pltpu.VMEM((tokens, QUERIES), jnp.bfloat16),
            pltpu.VMEM((tokens, HDS), jnp.float32),
            pltpu.VMEM((2 * HDS, tokens), jnp.bfloat16),
            pltpu.SemaphoreType.DMA((5,)),
        ],
        compiler_params=pltpu.CompilerParams(vmem_limit_bytes=32 << 20),
        cost_estimate=pl.CostEstimate(flops=100_000_000, bytes_accessed=1 << 18, transcendentals=0),
    )(place, store, *arrivals, pairs, inputs, *prior)


def pair_kernel(head, relays, place_ref, store_ref, *refs):
    count = 2 * relays
    arrivals = refs[:count]
    pair_ref, x_hbm, out_ref = refs[count:count + 3]
    panel, x_ref, q_ref, k_ref, turned, turned_t, exp_s, exp_t, mix, acc, grads, sems = refs[count + 3:]
    tokens = k_ref.shape[1]

    def start(source, b, part):
        pltpu.make_async_copy(source, panel.at[b, part], sems.at[b]).start()

    for b in range(2):
        @pl.when(place_ref[0, b] == 0)
        def _():
            for part in range(2):
                start(store_ref.at[place_ref[1, b], 0, part, :, pl.ds(head * HDT, HDT)], b, part)

        for d in range(relays):
            @pl.when(place_ref[0, b] == d + 1)
            def _():
                for part in range(2):
                    start(arrivals[2 * d + part].at[b], b, part)
    fetch = pltpu.make_async_copy(x_hbm, x_ref, sems.at[2])
    fetch.start()
    blocks = tokens // QUERIES
    halves = tokens // HALF
    pieces = HALF // PIECE
    rates = (LOG2E, HDT ** -0.5 * LOG2E)

    def prepare(b):
        pair = pair_ref[b, 0]
        q_ref[b] = pair[:, :HDS] * jnp.bfloat16(HDS ** -0.5)
        k_ref[b] = pair[:, HDS:]
        turned[b] = pair.T
        turned[b, :HDS] = turned[b, :HDS] * jnp.bfloat16(HDS ** -0.5)
        pltpu.make_async_copy(panel.at[b], panel.at[b], sems.at[b]).wait()
        turned_t[b] = panel[b, 0].T

    def exps(step, half):
        b, block = divmod(step, blocks)
        cols = pl.ds(block * QUERIES, QUERIES)
        rows = pl.ds(half * HALF, HALF)
        both = (dot(k_ref[b, rows, :], turned[b, :HDS, cols], NN), dot(panel[b, 1, rows, :], turned_t[b, :, cols], NN))
        stats = []
        for p in range(pieces):
            here = pl.ds(half * HALF + p * PIECE, PIECE)
            stat = []
            for score, rate, store in zip(both, rates, (exp_s, exp_t)):
                x = score[p * PIECE:(p + 1) * PIECE].reshape(PIECE // 8, 8, QUERIES)
                peak = jnp.max(x, axis=0)
                e = jnp.exp2((x - peak[None]) * rate)
                store[step % 2, here, :] = e.reshape(PIECE, QUERIES)
                stat.append((peak, jnp.sum(e, axis=0)))
            stats.append(stat)
        return stats

    def factors(stats):
        out = []
        for side in range(2):
            peaks = [stat[side][0] for stat in stats]
            top = peaks[0]
            for peak in peaks[1:]:
                top = jnp.maximum(top, peak)
            top = jnp.max(top, axis=0, keepdims=True)
            scale = [jnp.exp2((peak - top) * rates[side]) for peak in peaks]
            total = scale[0] * stats[0][side][1]
            for f, stat in zip(scale[1:], stats[1:]):
                total = total + f * stat[side][1]
            norm = 1.0 / jnp.sum(total, axis=0, keepdims=True)
            out.append([f * norm for f in scale])
        return out

    prepare(0)
    stats = [stat for half in range(halves) for stat in exps(0, half)]
    for step in range(2 * blocks):
        b, block = divmod(step, blocks)
        slot = step % 2
        cols = pl.ds(block * QUERIES, QUERIES)
        scale_s, scale_t = factors(stats)
        stats = []
        if step + 1 == blocks:
            prepare(1)
        for half in range(halves):
            if step + 1 < 2 * blocks:
                stats += exps(step + 1, half)
            for p in range(half * pieces, (half + 1) * pieces):
                here = pl.ds(p * PIECE, PIECE)
                s = exp_s[slot, here, :].reshape(PIECE // 8, 8, QUERIES) * scale_s[p][None]
                t = exp_t[slot, here, :].reshape(PIECE // 8, 8, QUERIES) * scale_t[p][None]
                mix[slot, here, :] = (s - t).reshape(PIECE, QUERIES).astype(jnp.bfloat16)
            rows = pl.ds(half * HALF, HALF)
            g = dot(mix[slot, rows, :], q_ref[b, cols, :], NN)
            if block == 0:
                acc[rows, :] = g
            else:
                acc[rows, :] += g
        gq = dot(turned[b, HDS:], mix[slot], NN) * HDS ** -0.5
        grads[:HDS, pl.ds(step * QUERIES, QUERIES)] = gq.astype(jnp.bfloat16)
        if block + 1 == blocks:
            grads[HDS:, pl.ds(b * tokens, tokens)] = acc[...].T.astype(jnp.bfloat16)
    fetch.wait()
    size = out_ref.shape[2]
    for d in range(out_ref.shape[0]):
        cols = pl.ds(d * size, size)
        out_ref[d] = (dot(grads[:, :tokens], x_ref[0, :, cols], NN)
                      + dot(grads[:, tokens:], x_ref[1, :, cols], NN))


def paired_grads(head, place, store, arrivals, pairs, inputs, data_ways):
    tokens, width = inputs.shape[1:]
    return pl.pallas_call(
        functools.partial(pair_kernel, head, len(arrivals) // 2),
        grid=(1,),
        out_shape=jax.ShapeDtypeStruct((data_ways, 2 * HDS, width // data_ways), jnp.float32),
        in_specs=[pl.BlockSpec(memory_space=pltpu.SMEM)]
        + [pl.BlockSpec(memory_space=pl.ANY)] * (1 + len(arrivals))
        + [
            pl.BlockSpec((2, 1, tokens, 2 * HDS), lambda u: (0, head, 0, 0)),
            pl.BlockSpec(memory_space=pl.ANY),
        ],
        out_specs=pl.BlockSpec((data_ways, 2 * HDS, width // data_ways), lambda u: (0, 0, 0)),
        scratch_shapes=[
            pltpu.VMEM((2, 2, tokens, HDT), jnp.bfloat16),
            pltpu.VMEM((2, tokens, width), jnp.bfloat16),
            pltpu.VMEM((2, tokens, HDS), jnp.bfloat16),
            pltpu.VMEM((2, tokens, HDS), jnp.bfloat16),
            pltpu.VMEM((2, 2 * HDS, tokens), jnp.bfloat16),
            pltpu.VMEM((2, HDT, tokens), jnp.bfloat16),
            pltpu.VMEM((2, tokens, QUERIES), jnp.float32),
            pltpu.VMEM((2, tokens, QUERIES), jnp.float32),
            pltpu.VMEM((2, tokens, QUERIES), jnp.bfloat16),
            pltpu.VMEM((tokens, HDS), jnp.float32),
            pltpu.VMEM((2 * HDS, 2 * tokens), jnp.bfloat16),
            pltpu.SemaphoreType.DMA((3,)),
        ],
        compiler_params=pltpu.CompilerParams(vmem_limit_bytes=32 << 20),
        cost_estimate=pl.CostEstimate(flops=100_000_000, bytes_accessed=1 << 18, transcendentals=0),
    )(place, store, *arrivals, pairs, inputs)


def projection_kernel(order_ref, own_ref, far_ref, near_ref, last_ref, x_ref, out_ref, weights):
    @pl.when(pl.program_id(0) == 0)
    def _():
        size = own_ref.shape[0]
        for r, rows in enumerate((own_ref, far_ref, near_ref, last_ref)):
            weights[pl.ds(pl.multiple_of(order_ref[r] * size, size), size), :] = rows[...]

    for c in range(out_ref.shape[1] // 2):
        pair = dot(x_ref[0], weights[:, 4 * c * HDS:4 * (c + 1) * HDS], NN).astype(jnp.bfloat16)
        out_ref[0, 2 * c] = pair[:, :2 * HDS]
        out_ref[0, 2 * c + 1] = pair[:, 2 * HDS:]


def pick_kernel(targets_ref, table_ref, out_ref, sem):
    cols = table_ref.shape[2]
    copies = [pltpu.make_async_copy(table_ref.at[targets_ref[h]], out_ref.at[:, pl.ds(h * cols, cols)], sem.at[h])
              for h in range(out_ref.shape[1] // cols)]
    for copy in copies:
        copy.start()
    for copy in copies:
        copy.wait()


def pick(table, targets):
    rows, cols = table.shape[1:]
    count = targets.shape[0]
    return pl.pallas_call(
        pick_kernel,
        in_specs=[pl.BlockSpec(memory_space=pltpu.SMEM), pl.BlockSpec(memory_space=pl.ANY)],
        out_specs=pl.BlockSpec(memory_space=pltpu.VMEM),
        out_shape=jax.ShapeDtypeStruct((rows, count * cols), table.dtype),
        scratch_shapes=[pltpu.SemaphoreType.DMA((count,))],
        cost_estimate=pl.CostEstimate(flops=0, bytes_accessed=1 << 20, transcendentals=0),
    )(targets, table)


def slots_kernel(targets_ref, first_ref, last_ref, out_ref):
    parts = [ref.at[h] for ref in (first_ref, last_ref) for h in range(ref.shape[0])]
    for s in range(out_ref.shape[0]):
        total = jnp.where(targets_ref[0] == s, parts[0][...], 0.0)
        for h in range(1, len(parts)):
            total = total + jnp.where(targets_ref[h] == s, parts[h][...], 0.0)
        out_ref[s] = total.astype(out_ref.dtype)


def add_slots(targets, first, last, count):
    return pl.pallas_call(
        slots_kernel,
        in_specs=[pl.BlockSpec(memory_space=pltpu.SMEM)] + [pl.BlockSpec(memory_space=pltpu.VMEM)] * 2,
        out_specs=pl.BlockSpec(memory_space=pltpu.VMEM),
        out_shape=jax.ShapeDtypeStruct((count, *first.shape[1:]), jnp.bfloat16),
        cost_estimate=pl.CostEstimate(flops=0, bytes_accessed=1 << 20, transcendentals=0),
    )(targets, first, last)


def project(inputs, block, data):
    near = [(d, d ^ 1) for d in range(4)]
    far = [(d, d ^ 2) for d in range(4)]
    across = lax.ppermute(block, "dp", far)
    beside = lax.ppermute(block, "dp", near)
    last = lax.ppermute(across, "dp", near)
    order = jnp.stack([data, data ^ 2, data ^ 1, data ^ 3])
    batches, tokens, width = inputs.shape
    rows, cols = block.shape
    return pl.pallas_call(
        projection_kernel,
        grid=(batches,),
        out_shape=jax.ShapeDtypeStruct((batches, cols // (2 * HDS), tokens, 2 * HDS), jnp.bfloat16),
        in_specs=[
            pl.BlockSpec(memory_space=pltpu.SMEM),
            *[pl.BlockSpec((rows, cols), lambda b: (0, 0))] * 4,
            pl.BlockSpec((1, tokens, width), lambda b: (b, 0, 0)),
        ],
        out_specs=pl.BlockSpec((1, cols // (2 * HDS), tokens, 2 * HDS), lambda b: (b, 0, 0, 0)),
        scratch_shapes=[pltpu.VMEM((width, cols), jnp.bfloat16)],
        compiler_params=pltpu.CompilerParams(vmem_limit_bytes=40 << 20),
        cost_estimate=pl.CostEstimate(flops=4_000_000_000, bytes_accessed=8 << 20, transcendentals=0),
    )(order, block, across, beside, last, inputs)


def body(teacher_panels, owner_plan, head_map, student_input, student_weights):
    model_ways = lax.axis_size("mp")
    data_ways = lax.axis_size("dp")
    groups = lax.axis_size("group")
    column = lax.axis_index("mp")
    data = lax.axis_index("dp")
    store_slots = teacher_panels.shape[0]
    tokens = teacher_panels.shape[3]
    heads = teacher_panels.shape[4] // HDT
    width = student_input.shape[-1]
    row_block = width // data_ways
    column_block = width // model_ways
    column_heads = column_block // HDS
    targets = lax.dynamic_slice_in_dim(head_map[:, 0], column * heads, heads)

    here = lax.axis_index("group")
    owner = owner_plan // store_slots
    dist = jnp.where(data % 2 == 0, here - owner, owner - here) % groups
    slot = owner_plan % store_slots
    place = jnp.stack([dist, slot])
    ring = [(z * data_ways + d, (z + (1 if d % 2 == 0 else -1)) % groups * data_ways + d)
            for z in range(groups) for d in range(data_ways)]

    def held(store, part, start, count):
        pick = [lax.dynamic_slice(store, (slot[b], 0, part, 0, start), (1, 1, 1, tokens, count)) for b in range(2)]
        return jnp.concatenate(pick)[:, 0, 0]

    first = [held(teacher_panels, chunk, 0, HDT) for chunk in range(LAG)]
    first, student_weights, store = lax.optimization_barrier((first, student_weights, teacher_panels))

    table = student_weights[0].reshape(2, row_block, column_heads, HDS).transpose(2, 1, 0, 3)
    table = table.reshape(1, column_heads, row_block, 2 * HDS)
    table = lax.all_to_all(jnp.broadcast_to(table, (model_ways, *table.shape[1:])), "mp", 0, 0, tiled=True)

    own = [held(store, part, HDT, (heads - 1) * HDT) for part in range(2)]
    chunks = 2 * heads
    stages = chunks + LAG * (groups - 2)
    lead = 1 + LAG * (groups - 2)
    inputs = student_input[0, :, 0]
    arrived = []
    pairs = None
    pieces = []

    def sources(head):
        return [arrived[2 * head + part + LAG * d] for d in range(groups - 1) for part in range(2)]

    def grad(unit, place):
        head, b = divmod(unit, 2)
        return relation_grads(head, b, place, teacher_panels, sources(head), pairs, inputs, pieces[-1:] * b, data_ways)

    for stage in range(stages):
        if stage < LAG:
            send = first[stage]
        else:
            passed = arrived[stage - LAG]
            if stage == LAG + 1:
                passed, table, own = lax.optimization_barrier((passed, table, own))
                mine = pick(table.reshape(model_ways * column_heads, row_block, 2 * HDS), targets)
                pairs = project(inputs, mine, data)
            head, part = divmod(min(stage, chunks - 1), 2)
            mine = own[part][:, :, (head - 1) * HDT:head * HDT]
            send = jnp.where((dist == 0)[:, None, None], mine, passed)
            send, own = lax.optimization_barrier((send, own))
        unit = stage - lead - LAG - 1
        if unit >= 0:
            piece, send, place = lax.optimization_barrier((grad(unit, place), send, place))
            pieces.append(piece)
        arrived.append(lax.ppermute(send, ("group", "dp"), ring))
    early = len(pieces) // 2
    reduced = reduce_data(pieces[1::2], data, jnp.float32)
    final = []
    for head in range(early, heads):
        if head == heads - 1:
            reduced, place = lax.optimization_barrier((reduced, place))
        piece = paired_grads(head, place, teacher_panels, sources(head), pairs, inputs, data_ways)
        piece, place = lax.optimization_barrier((piece, place))
        final.append(piece)

    final = reduce_data(final, data, jnp.bfloat16)
    slots = add_slots(targets, reduced, final, model_ways * column_heads)
    slots = slots.reshape(model_ways, column_heads, 2 * HDS, row_block)
    slots = lax.all_to_all(slots, "mp", 0, 0, tiled=True)
    result = jnp.sum(slots.astype(jnp.float32), axis=0).reshape(column_heads, 2, HDS, row_block)
    return result.transpose(1, 3, 0, 2).reshape(1, 2, row_block, column_block)


def reduce_data(pieces, data, dtype):
    near = [(d, d ^ 1) for d in range(4)]
    far = [(d, d ^ 2) for d in range(4)]
    core = data % 2
    chip = data // 2
    halves = [piece.reshape(2, 2, *piece.shape[1:]) for piece in pieces]

    def half(which):
        return jnp.stack([lax.dynamic_index_in_dim(piece, which, 1, keepdims=False) for piece in halves], axis=1)

    kept = half(core) + lax.ppermute(half(1 - core), "dp", near)
    got = lax.ppermute(lax.dynamic_index_in_dim(kept, 1 - chip, 0, keepdims=False).astype(dtype), "dp", far)
    return lax.dynamic_index_in_dim(kept, chip, 0, keepdims=False) + got.astype(jnp.float32)


def solution(mesh):
    in_specs = (
        P("group", "dp", None, None, "mp"),
        P(),
        P(),
        P("group", None, "dp", None, None),
        P("group", None, "dp", "mp"),
    )
    out_specs = P("group", None, "dp", "mp")
    return jax.shard_map(body, mesh=mesh, in_specs=in_specs, out_specs=out_specs, check_vma=False)
```
